512 devices in a mesh: dop: 16 (over y, core), rng: 32 (over x, z).
Axes of the slice: x: 4, y: 8, z: 8, core: 2. Of those that a mesh axis runs over, the one named last changes fastest.
Arguments:
- radar_cube: bfloat16 [2, 128, 2048, 512], P(None, 'dop', 'rng'), may hold values from -40 to 40
- train_gates: int32 [16, 1536], P('dop', 'rng'), may hold values from 0 to 63, as said below
- look_angles: int32 [16, 8], P('dop'), may hold values from 0 to 255
Outputs:
- filtered: float32 [2, 16, 8, 2048], P(None, 'dop', None, 'rng')
The draws below stay inside these ranges and needn't reach their ends.
Inputs may be any that keep to these rules, and one draw needn't show every extreme that they name: `train_gates`: entries k * 48 to (k + 1) * 48 - 1 of a bin's row list in increasing order the gates of the k-th block of 64 consecutive range gates, counted from that block's first gate, that lie outside one run of 16 consecutive gates of the block.
All inputs are finite; a program needn't handle non-finite values.
Results may differ from the reference program's by a relative error of at most 0.014.
The reference program's roundings to bfloat16 on the way count: a program that leaves them out, or rounds other values in their place, can miss the bound.
Values may be sent and summed in bfloat16 or wider, within the bound.
A program may use at most 64 MiB of HBM per device.

```python
import math
import jax
import jax.numpy as jnp
from jax import lax

C = 512
P_SIZE = 128
NANG = 256
BEAMS = 8
G_DEV = 64
GUARD = 16
TR_DEV = 48
NB = 16
GATES = 2048
TRAIN = 1536


def draw_radar_cube(key, part):
    subkeys = jax.random.split(key, 5)
    source_count = 16
    gains = jnp.exp(jax.random.uniform(subkeys[0], (C,), minval=math.log(0.5), maxval=math.log(2.0)))
    directions = jax.random.uniform(subkeys[1], (source_count,), minval=-1.0, maxval=1.0)
    powers = jnp.exp(jax.random.uniform(subkeys[2], (source_count,), minval=math.log(0.5), maxval=math.log(4.0))) * (6.0 / source_count)
    phase = math.pi * jnp.arange(C, dtype=jnp.float32)[:, None] * directions[None, :]
    steer_real = jnp.cos(phase)
    steer_imag = jnp.sin(phase)
    amplitude = jax.random.normal(subkeys[3], (2, P_SIZE, GATES, source_count), dtype=jnp.float32) * jnp.sqrt(powers / 2.0)
    clutter_real = jnp.einsum('pgk,ck->pgc', amplitude[0], steer_real) - jnp.einsum('pgk,ck->pgc', amplitude[1], steer_imag)
    clutter_imag = jnp.einsum('pgk,ck->pgc', amplitude[0], steer_imag) + jnp.einsum('pgk,ck->pgc', amplitude[1], steer_real)
    clutter = jnp.stack([clutter_real, clutter_imag])
    noise = jax.random.normal(subkeys[4], (2, P_SIZE, GATES, C), dtype=jnp.float32)
    samples = (noise + clutter) * gains[None, None, None, :]
    return jnp.clip(samples, -40.0, 40.0).astype(jnp.bfloat16)


def draw_train_gates(key, part):
    block_count = TRAIN // TR_DEV
    starts = jax.random.randint(key, (NB, block_count, 1), 0, G_DEV - GUARD + 1)
    offsets = jnp.arange(TR_DEV, dtype=jnp.int32)[None, None, :]
    gate_index = offsets + GUARD * (offsets >= starts).astype(jnp.int32)
    return gate_index.reshape(NB, TRAIN).astype(jnp.int32)


def set_ends(result, own_key, smallest, largest):
    shape = result.shape
    spot = [jax.random.randint(jax.random.fold_in(own_key, axis), (), 0, shape[axis]) for axis in range(len(shape))]
    result = result.at[tuple(spot)].set(smallest)
    longest = shape.index(max(shape))
    spot[longest] = (spot[longest] + 1) % shape[longest]
    return result.at[tuple(spot)].set(largest)


def setup_inputs(seed: int = 0) -> dict:
    streams_of = jax.random.split(jax.random.key(seed), 4)
    return {
        "radar_cube": draw_radar_cube(jax.random.fold_in(streams_of[3], 71), 0),
        "train_gates": draw_train_gates(jax.random.fold_in(streams_of[3], 71), 0),
        "look_angles": set_ends(jax.random.randint(streams_of[2], (NB, BEAMS), 0, NANG), jax.random.fold_in(streams_of[2], 1), 0, NANG - 1).astype(jnp.int32),
    }


load_eps = 1e-05

def doppler_table(bin_count, pulses):
    bin_freq = jnp.arange(bin_count, dtype=jnp.int32) * (pulses // bin_count)
    pulse_index = jnp.arange(pulses, dtype=jnp.int32)
    phase = (bin_freq[:, None] * pulse_index[None, :] % pulses).astype(jnp.float32) * (2.0 * math.pi / pulses)
    cosine = jnp.cos(phase).astype(jnp.bfloat16)
    sine = jnp.sin(phase).astype(jnp.bfloat16)
    upper = jnp.concatenate([cosine, sine], 1)
    lower = jnp.concatenate([-sine, cosine], 1)
    return jnp.concatenate([upper, lower], 0)

def gram_terms(train_rows):
    real_part = train_rows[0]
    imag_part = train_rows[1]
    contract = (((0,), (0,)), ((), ()))
    stacked = jnp.concatenate([real_part, imag_part], 0)
    power_sum = lax.dot_general(stacked.astype(jnp.float32), stacked.astype(jnp.float32), contract, preferred_element_type=jnp.float32)
    left_rows = jnp.concatenate([real_part, -imag_part], 0)
    right_rows = jnp.concatenate([imag_part, real_part], 0)
    cross_sum = lax.dot_general(left_rows.astype(jnp.float32), right_rows.astype(jnp.float32), contract, preferred_element_type=jnp.float32)
    return (power_sum, cross_sum)

def solve_weights(power_sum, cross_sum, look_row, train_count, angle_count):
    channels = power_sum.shape[0]
    top_half = jnp.concatenate([power_sum, cross_sum], 1)
    bottom_half = jnp.concatenate([cross_sum.T, power_sum], 1)
    covariance = jnp.concatenate([top_half, bottom_half], 0) / train_count
    loading = load_eps * jnp.trace(covariance) / (2 * channels)
    covariance = covariance + loading * jnp.eye(2 * channels, dtype=jnp.float32)
    factor = jnp.linalg.cholesky(covariance)
    channel_index = jnp.arange(channels, dtype=jnp.int32)
    slope = 2 * look_row.astype(jnp.int32) + 1 - angle_count
    modulus = channel_index[:, None] * slope[None, :] % (2 * angle_count)
    phase = modulus.astype(jnp.float32) * (math.pi / angle_count)
    steering = jnp.concatenate([jnp.cos(phase), jnp.sin(phase)], 0)
    whitened = jax.scipy.linalg.solve_triangular(factor, steering, lower=True)
    lengths = jnp.sqrt(lax.optimization_barrier(jnp.sum(whitened * whitened, axis=0)))
    weights = jax.scipy.linalg.solve_triangular(factor, whitened / lengths[None, :], trans=1, lower=True)
    return weights.astype(jnp.bfloat16)

def filter_gates(spectrum, weights):
    direct = jnp.concatenate([spectrum[0], spectrum[1]], 1)
    rotated = jnp.concatenate([-spectrum[1], spectrum[0]], 1)
    contract = (((0,), (1,)), ((), ()))
    real_out = lax.dot_general(weights.astype(jnp.float32), direct.astype(jnp.float32), contract, preferred_element_type=jnp.float32)
    imag_out = lax.dot_general(weights.astype(jnp.float32), rotated.astype(jnp.float32), contract, preferred_element_type=jnp.float32)
    return jnp.stack([real_out, imag_out])

def reference(radar_cube, train_gates, look_angles):
    dft_table = doppler_table(NB, P_SIZE)
    flattened = radar_cube.reshape(2 * P_SIZE, GATES * C)
    spectral = (jnp.dot(dft_table.astype(jnp.float32), flattened.astype(jnp.float32), preferred_element_type=jnp.float32) * (1.0 / math.sqrt(P_SIZE))).astype(jnp.bfloat16)
    spectral = spectral.reshape(2, NB, GATES, C)
    block_offset = jnp.arange(TRAIN, dtype=jnp.int32) // TR_DEV * G_DEV

    def per_bin(bin_index):
        spectrum = spectral[:, bin_index]
        gate_list = train_gates[bin_index].astype(jnp.int32) + block_offset
        train_rows = jnp.take(spectrum, gate_list, axis=1)
        power_sum, cross_sum = gram_terms(train_rows)
        weights = solve_weights(power_sum, cross_sum, look_angles[bin_index], TRAIN, NANG)
        return filter_gates(spectrum, weights)
    outcome = lax.map(per_bin, jnp.arange(NB, dtype=jnp.int32))
    return jnp.transpose(outcome, (1, 0, 2, 3))
```

```python
import functools
import math

import jax
import jax.numpy as jnp
import numpy as np
from jax import lax
from jax.experimental import pallas as pl
from jax.experimental.pallas import tpu as pltpu
from jax.sharding import PartitionSpec as P

F32 = jnp.float32
BF16 = jnp.bfloat16
HIGH = lax.Precision.HIGHEST
MESH = pl.DeviceIdType.MESH
PULSES = 128
NANG = 256
BEAMS = 8
LOAD = 1e-05
DOP = 16
NX = 4
NZ = 8
SIDE = 128


def twiddles():
    angle = 2.0 * math.pi * np.arange(16) / 16
    rounded = lambda v: np.round(v, 12).astype(BF16).astype(np.float32)
    return rounded(np.cos(angle)), rounded(np.sin(angle))


def gather_kernel(cube, gates, full, spec, got, send, even, odd, rows, part, shares,
                  own_sem, a_send, a_recv, b_send, b_recv, x_send, x_recv, r_send, r_recv,
                  z_send, z_recv, f_send, f_recv):
    dop = lax.axis_index("dop")
    rng = lax.axis_index("rng")
    x, z = rng // NZ, lax.rem(rng, NZ)

    def dop_peer(step):
        return {"dop": lax.rem(dop + step, DOP)}

    def x_peer(step):
        return {"rng": lax.rem(x + step, NX) * NZ + z}

    def z_peer(step):
        return {"rng": x * NZ + lax.rem(z + step, NZ)}

    barrier = pltpu.get_barrier_semaphore()

    def greet(peer, count):
        def one(step, carry):
            pl.semaphore_signal(barrier, inc=1, device_id=peer(step), device_id_type=MESH)
            return carry
        lax.fori_loop(1, count, one, 0)

    greet(dop_peer, DOP)
    greet(x_peer, NX)
    greet(z_peer, NZ)
    pl.semaphore_wait(barrier, DOP + NX + NZ - 3)

    def tile_of(index):
        return (pl.ds(pl.multiple_of(index // 4 * 16, 16), 16),
                pl.ds(pl.multiple_of(lax.rem(index, 4) * 128, 128), 128))

    def loop(count, body):
        def one(step, carry):
            body(step)
            return carry
        lax.fori_loop(1, count, one, 0)

    def a_copy(step):
        g, c = tile_of(lax.rem(dop + step, DOP))
        return pltpu.make_async_remote_copy(
            src_ref=cube.at[:, :, g, c], dst_ref=got.at[step], send_sem=a_send.at[step],
            recv_sem=a_recv.at[step], device_id=dop_peer(step), device_id_type=MESH)

    loop(DOP, lambda step: a_copy(step).start())
    g, c = tile_of(dop)
    own = pltpu.make_async_copy(cube.at[:, :, g, c], got.at[0], own_sem)
    own.start()
    own.wait()
    sign = jnp.where(lax.rem(dop, 2) == 0, 1.0, -1.0).astype(F32)
    first = got[0].astype(F32)
    even[...] = first
    odd[...] = sign * first

    def fold(step):
        a_copy(step).wait_recv()
        block = got[step].astype(F32)
        flip = jnp.where(lax.rem(step, 2) == 0, sign, -sign)
        even[...] += block
        odd[...] += flip * block

    loop(DOP, fold)

    cosine, sine = twiddles()
    norm = 1.0 / math.sqrt(PULSES)
    for half in range(2):
        rows8 = slice(8 * half, 8 * half + 8)
        for parity, source in enumerate((even, odd)):
            re = [source[0, q, rows8, :] for q in range(8)]
            im = [source[1, q, rows8, :] for q in range(8)]
            for b in range(parity, DOP, 2):
                up = low = None
                for q in range(8):
                    cb, sb = float(cosine[b * q % 16]), float(sine[b * q % 16])
                    terms_up = [t for t in ((cb, re[q]), (sb, im[q])) if t[0] != 0.0]
                    terms_low = [t for t in ((-sb, re[q]), (cb, im[q])) if t[0] != 0.0]
                    for k, v in terms_up:
                        up = k * v if up is None else up + k * v
                    for k, v in terms_low:
                        low = k * v if low is None else low + k * v
                even_out = (up * norm, low * norm)
                for i in range(2):
                    part[i * 16 + b, rows8, 0:128] = even_out[i]
    for b in range(DOP):
        for i in range(2):
            send[b, i] = part[i * 16 + b, :, 0:128].astype(BF16)

    def b_copy(step):
        return pltpu.make_async_remote_copy(
            src_ref=send.at[lax.rem(dop + step, DOP)], dst_ref=spec.at[:, g, c], send_sem=b_send.at[step],
            recv_sem=b_recv.at[step], device_id=dop_peer(step), device_id_type=MESH)

    loop(DOP, lambda step: b_copy(step).start())
    spec[:, g, c] = send[dop]
    loop(DOP, lambda step: b_copy(step).wait_recv())

    gate = lax.broadcasted_iota(jnp.int32, (64, 48), 0)
    hit = jnp.where(gate == gates[...], 1.0, 0.0)
    mask = jnp.max(hit, axis=1, keepdims=True)
    for i in range(2):
        rows[0, i] = (spec[i].astype(F32) * mask).astype(BF16)

    def x_copy(step):
        return pltpu.make_async_remote_copy(
            src_ref=rows.at[0], dst_ref=rows.at[step], send_sem=x_send.at[step],
            recv_sem=x_recv.at[step], device_id=x_peer(step), device_id_type=MESH)

    loop(NX, lambda step: x_copy(step).start())
    loop(NX, lambda step: x_copy(step).wait_recv())

    def columns(block):
        lanes = pl.ds(pl.multiple_of(block * SIDE, SIDE), SIDE)
        return (rows[:, 0, :, lanes].reshape(256, SIDE), rows[:, 1, :, lanes].reshape(256, SIDE))

    def dot(a, b):
        return lax.dot_general(a, b, (((0,), (0,)), ((), ())), preferred_element_type=F32)

    def power(a, b):
        return dot(a[0], b[0]) + dot(a[1], b[1])

    def cross(a, b):
        return dot(a[0], b[1]) - dot(a[1], b[0])

    near, far = lax.rem(x + 1, NX), lax.rem(x + 2, NX)
    mine = columns(x)
    low1, high1 = columns(jnp.minimum(x, near)), columns(jnp.maximum(x, near))
    low2, high2 = columns(jnp.minimum(x, far)), columns(jnp.maximum(x, far))
    lower = lax.broadcasted_iota(jnp.int32, (SIDE, SIDE), 0) >= lax.broadcasted_iota(jnp.int32, (SIDE, SIDE), 1)
    tiles = (jnp.where(lower, power(mine, mine), cross(mine, mine)), power(low1, high1), cross(low1, high1),
             jnp.where(x < 2, power(low2, high2), cross(low2, high2)))
    for t in range(4):
        for k in range(NZ):
            shares_rows = slice(16 * k, 16 * k + 16)
            part[k, :, 128 * t:128 * t + 128] = tiles[t][shares_rows]

    def r_copy(step):
        return pltpu.make_async_remote_copy(
            src_ref=part.at[lax.rem(z + step, NZ)], dst_ref=shares.at[step], send_sem=r_send.at[step],
            recv_sem=r_recv.at[step], device_id=z_peer(step), device_id_type=MESH)

    loop(NZ, lambda step: r_copy(step).start())
    shares[0] = part[z]

    loop(NZ, lambda step: r_copy(step).wait_recv())
    total = shares[0]
    for step in range(1, NZ):
        total = total + shares[step]
    strip = pl.ds(pl.multiple_of(z * 16, 16), 16)
    full[x, strip, :] = total * (1.0 / 1536.0)

    def z_copy(step):
        return pltpu.make_async_remote_copy(
            src_ref=full.at[x, strip], dst_ref=full.at[x, strip], send_sem=z_send.at[step],
            recv_sem=z_recv.at[step], device_id=z_peer(step), device_id_type=MESH)

    loop(NZ, lambda step: z_copy(step).start())
    loop(NZ, lambda step: z_copy(step).wait_recv())

    def f_copy(step):
        return pltpu.make_async_remote_copy(
            src_ref=full.at[x], dst_ref=full.at[x], send_sem=f_send.at[step],
            recv_sem=f_recv.at[step], device_id=x_peer(step), device_id_type=MESH)

    loop(NX, lambda step: f_copy(step).start())
    loop(NX, lambda step: f_copy(step).wait_recv())

    loop(DOP, lambda step: a_copy(step).wait_send())
    loop(DOP, lambda step: b_copy(step).wait_send())
    loop(NX, lambda step: x_copy(step).wait_send())
    loop(NZ, lambda step: r_copy(step).wait_send())
    loop(NZ, lambda step: z_copy(step).wait_send())
    loop(NX, lambda step: f_copy(step).wait_send())


def gather(cube, gates):
    dma = pltpu.SemaphoreType.DMA
    return pl.pallas_call(
        gather_kernel,
        out_shape=(jax.ShapeDtypeStruct((4, SIDE, 512), F32), jax.ShapeDtypeStruct((2, 64, 512), BF16)),
        in_specs=[pl.BlockSpec(memory_space=pl.ANY), pl.BlockSpec(memory_space=pltpu.VMEM)],
        out_specs=(pl.BlockSpec(memory_space=pltpu.VMEM),) * 2,
        scratch_shapes=[
            pltpu.VMEM((DOP, 2, 8, 16, 128), BF16),
            pltpu.VMEM((DOP, 2, 16, 128), BF16),
            pltpu.VMEM((2, 8, 16, 128), F32),
            pltpu.VMEM((2, 8, 16, 128), F32),
            pltpu.VMEM((NX, 2, 64, 512), BF16),
            pltpu.VMEM((32, 16, 512), F32),
            pltpu.VMEM((NZ, 16, 512), F32),
            dma(()),
            dma((DOP,)), dma((DOP,)), dma((DOP,)), dma((DOP,)), dma((NX,)), dma((NX,)), dma((NZ,)), dma((NZ,)),
            dma((NZ,)), dma((NZ,)), dma((NX,)), dma((NX,)),
        ],
        compiler_params=pltpu.CompilerParams(collective_id=0, has_side_effects=True, vmem_limit_bytes=32 << 20),
        cost_estimate=pl.CostEstimate(flops=10**9, bytes_accessed=10**7, transcendentals=0),
    )(cube, gates)


def parts3(x):
    a = x.astype(BF16).astype(F32)
    r = x - a
    b = r.astype(BF16).astype(F32)
    c = (r - b).astype(BF16).astype(F32)
    return a, b, c

def left6(t):
    a, b, c = t
    return [a, a, b, a, b, c]

def right6(t):
    a, b, c = t
    return [a, b, a, c, b, a]

def neg(t):
    return tuple(-v for v in t)

def invert_block(dr, di):
    lane = lax.broadcasted_iota(jnp.int32, (8, 128), 1)
    sub = lax.broadcasted_iota(jnp.int32, (8, 128), 0)
    wide = lax.broadcasted_iota(jnp.int32, (128, 128), 1)
    for p in range(16):
        o = 8 * p
        rr, ri = dr[o:o+8, :], di[o:o+8, :]
        cr = [jnp.broadcast_to(rr[:, o+j:o+j+1], (8, 128)) for j in range(8)]
        ci = [jnp.broadcast_to(ri[:, o+j:o+j+1], (8, 128)) for j in range(8)]
        inside = (lane >= o) & (lane < o + 8)
        xr = jnp.where(inside, jnp.where(lane == o + sub, 1.0, 0.0), rr)
        xi = jnp.where(inside, 0.0, ri)
        for i in range(8):
            inv = 1.0 / cr[i][i:i+1, :]
            here = sub == i
            def step(vr, vi):
                tr = vr[i:i+1, :] * inv
                ti = vi[i:i+1, :] * inv
                nr = jnp.where(here, tr, vr - (cr[i] * tr - ci[i] * ti))
                ni = jnp.where(here, ti, vi - (cr[i] * ti + ci[i] * tr))
                return nr, ni
            for j in range(i + 1, 8):
                cr[j], ci[j] = step(cr[j], ci[j])
            xr, xi = step(xr, xi)
        sign = jnp.where(lane < o, -1.0, 1.0)
        a, b = parts3(sign * rr), parts3(-sign * ri)
        left = jnp.concatenate(left6(a) + left6(b), 0).astype(BF16)
        u, v = parts3(xr), parts3(xi)
        right = jnp.concatenate([
            jnp.concatenate(right6(u) + right6(neg(v)), 0),
            jnp.concatenate(right6(v) + right6(u), 0)], 1).astype(BF16)
        upd = lax.dot_general(left, right, (((0,), (0,)), ((), ())), preferred_element_type=F32)
        hole = (wide >= o) & (wide < o + 8)
        dr[...] = jnp.where(hole, 0.0, dr[...]) - upd[:, :128]
        di[...] = jnp.where(hole, 0.0, di[...]) - upd[:, 128:]
        dr[o:o+8, :] = xr
        di[o:o+8, :] = xi

def solve_body(tiles_ref, steer_ref, spec_ref, out_ref, dr, di, row, w, x):
    eye = lax.broadcasted_iota(jnp.int32, (128, 128), 0) - lax.broadcasted_iota(jnp.int32, (128, 128), 1)
    tr = 0.0
    for i in range(4):
        tr = tr + jnp.sum(jnp.where(eye == 0, tiles_ref[i, :, 0:128], 0.0))
    load = LOAD * tr / 512.0
    def off(i, j):
        if j - i == 1:
            return (i, 1), (i, 2)
        if j - i == 3:
            return (3, 1), (3, 2)
        return (i, 3), (i + 2, 3)
    for i in range(4):
        for j in range(i + 1, 4):
            (a, b), (c, d) = off(i, j)
            row[i, 0:128, 128*j:128*j+128] = tiles_ref[a, :, 128*b:128*b+128]
            row[i, 128:256, 128*j:128*j+128] = -tiles_ref[c, :, 128*d:128*d+128]
        t = tiles_ref[i, :, 0:128]
        tt = t.T
        row[i, 0:128, 128*i:128*i+128] = jnp.where(eye > 0, t, tt) + jnp.where(eye == 0, load, 0.0)
        row[i, 128:256, 128*i:128*i+128] = jnp.where(eye > 0, tt, jnp.where(eye < 0, -t, 0.0))
        row[i, 0:128, 512:640] = steer_ref[0, 128*i:128*i+128, :]
        row[i, 128:256, 512:640] = steer_ref[1, 128*i:128*i+128, :]

    def body(k, _):
        dr[...] = jnp.zeros_like(dr)
        for kk in range(4):
            @pl.when(k == kk)
            def _():
                dr[...] = row[kk, 0:128, 128*kk:128*kk+128]
                di[...] = row[kk, 128:256, 128*kk:128*kk+128]
        invert_block(dr, di)
        for kk in range(4):
            @pl.when(k == kk)
            def _():
                s = 128 * (kk + 1)
                a, b = dr[...], di[...]
                emb = jnp.concatenate([jnp.concatenate([a, -b], 1), jnp.concatenate([b, a], 1)], 0)
                w[kk, :, s:640] = jnp.dot(emb, row[kk, :, s:640], preferred_element_type=F32, precision=HIGH)
                for i in range(kk + 1, 4):
                    c = 128 * i
                    lhs = row[kk, :, c:c+128]
                    wr = w[kk, 0:128, c:640]
                    wi = w[kk, 128:256, c:640]
                    both = jnp.concatenate([jnp.concatenate([wr, wi], 1), jnp.concatenate([wi, -wr], 1)], 0)
                    n = 640 - c
                    u = lax.dot_general(lhs, both, (((0,), (0,)), ((), ())), preferred_element_type=F32, precision=HIGH)
                    row[i, 0:128, c:640] -= u[:, :n]
                    row[i, 128:256, c:640] -= u[:, n:]
        return 0
    lax.fori_loop(0, 4, body, 0)
    q = jnp.zeros((1, 128), F32)
    for k in (3, 2, 1, 0):
        y = w[k, :, 512:640]
        for j in range(k + 1, 4):
            wr = w[k, 0:128, 128*j:128*j+128]
            wi = w[k, 128:256, 128*j:128*j+128]
            emb = jnp.concatenate([jnp.concatenate([wr, -wi], 1), jnp.concatenate([wi, wr], 1)], 0)
            y = y - jnp.dot(emb, x[j], preferred_element_type=F32, precision=HIGH)
        x[k] = y
        for h in range(2):
            q = q + jnp.sum(y[128*h:128*h+128] * steer_ref[h, 128*k:128*k+128, :], axis=0, keepdims=True)
    lanes = lax.broadcasted_iota(jnp.int32, (1, 128), 1)
    scale = jnp.where(lanes < BEAMS, lax.rsqrt(jnp.where(lanes < BEAMS, q, 1.0)), 0.0)
    re = jnp.zeros((64, 128), F32)
    im = jnp.zeros((64, 128), F32)
    wr = jnp.concatenate([x[k, 0:128] for k in range(4)], 0)
    wi = jnp.concatenate([x[k, 128:256] for k in range(4)], 0)
    wr = (wr * scale).astype(BF16)
    wi = (wi * scale).astype(BF16)
    sr, si = spec_ref[0], spec_ref[1]
    dot = functools.partial(jnp.dot, preferred_element_type=F32)
    re = dot(sr, wr) + dot(si, wi)
    im = dot(sr, wi) - dot(si, wr)
    out_ref[0] = re.T[0:8]
    out_ref[1] = im.T[0:8]

SCR = [pltpu.VMEM((128,128),F32), pltpu.VMEM((128,128),F32), pltpu.VMEM((4,256,640),F32), pltpu.VMEM((4,256,640),F32), pltpu.VMEM((4,256,128),F32)]
def solve(tiles, steer, spec):
    return pl.pallas_call(solve_body, out_shape=jax.ShapeDtypeStruct((2,8,64),F32),
       in_specs=[pl.BlockSpec(memory_space=pltpu.VMEM)]*3, out_specs=pl.BlockSpec(memory_space=pltpu.VMEM),
       scratch_shapes=SCR, compiler_params=pltpu.CompilerParams(vmem_limit_bytes=48<<20))(tiles, steer, spec)


def on_device(radar_cube, train_gates, look_angles):
    full, spec = gather(radar_cube, train_gates)
    channel = jnp.arange(512, dtype=jnp.int32)
    slope = 2 * look_angles[0] + 1 - NANG
    phase = (channel[:, None] * slope[None, :] % (2 * NANG)).astype(F32) * (math.pi / NANG)
    steering = jnp.stack([jnp.cos(phase), jnp.sin(phase)])
    steering = jnp.pad(steering, ((0, 0), (0, 0), (0, 128 - BEAMS)))
    return solve(full, steering, spec)[:, None]


def solution(mesh):
    return jax.shard_map(
        on_device,
        mesh=mesh,
        in_specs=(P(None, "dop", "rng", None), P("dop", "rng"), P("dop", None)),
        out_specs=P(None, "dop", None, "rng"),
        check_vma=False,
    )
```

```python
import functools
import math

import jax
import jax.numpy as jnp
import numpy as np
from jax import lax
from jax.experimental import pallas as pl
from jax.experimental.pallas import tpu as pltpu
from jax.sharding import PartitionSpec as P

F32 = jnp.float32
BF16 = jnp.bfloat16
HIGH = lax.Precision.HIGHEST
MESH = pl.DeviceIdType.MESH
PULSES = 128
NANG = 256
BEAMS = 8
LOAD = 1e-05
DOP = 16
NX = 4
NZ = 8
RNG = NX * NZ
SIDE = 128
TRAIN = 1536
ROOTS = (0, 20)


def twiddles():
    angle = 2.0 * math.pi * np.arange(16) / 16
    rounded = lambda v: np.round(v, 12).astype(BF16).astype(np.float32)
    return rounded(np.cos(angle)), rounded(np.sin(angle))


def parts3(x):
    a = x.astype(BF16).astype(F32)
    r = x - a
    b = r.astype(BF16).astype(F32)
    c = (r - b).astype(BF16).astype(F32)
    return a, b, c

def left6(t):
    a, b, c = t
    return [a, a, b, a, b, c]

def right6(t):
    a, b, c = t
    return [a, b, a, c, b, a]

def neg(t):
    return tuple(-v for v in t)

def invert_block(dr, di):
    lane = lax.broadcasted_iota(jnp.int32, (8, 128), 1)
    sub = lax.broadcasted_iota(jnp.int32, (8, 128), 0)
    wide = lax.broadcasted_iota(jnp.int32, (128, 128), 1)
    for p in range(16):
        o = 8 * p
        rr, ri = dr[o:o+8, :], di[o:o+8, :]
        cr = [jnp.broadcast_to(rr[:, o+j:o+j+1], (8, 128)) for j in range(8)]
        ci = [jnp.broadcast_to(ri[:, o+j:o+j+1], (8, 128)) for j in range(8)]
        inside = (lane >= o) & (lane < o + 8)
        xr = jnp.where(inside, jnp.where(lane == o + sub, 1.0, 0.0), rr)
        xi = jnp.where(inside, 0.0, ri)
        for i in range(8):
            inv = 1.0 / cr[i][i:i+1, :]
            here = sub == i
            def step(vr, vi):
                tr = vr[i:i+1, :] * inv
                ti = vi[i:i+1, :] * inv
                nr = jnp.where(here, tr, vr - (cr[i] * tr - ci[i] * ti))
                ni = jnp.where(here, ti, vi - (cr[i] * ti + ci[i] * tr))
                return nr, ni
            for j in range(i + 1, 8):
                cr[j], ci[j] = step(cr[j], ci[j])
            xr, xi = step(xr, xi)
        sign = jnp.where(lane < o, -1.0, 1.0)
        a, b = parts3(sign * rr), parts3(-sign * ri)
        left = jnp.concatenate(left6(a) + left6(b), 0).astype(BF16)
        u, v = parts3(xr), parts3(xi)
        right = jnp.concatenate([
            jnp.concatenate(right6(u) + right6(neg(v)), 0),
            jnp.concatenate(right6(v) + right6(u), 0)], 1).astype(BF16)
        upd = lax.dot_general(left, right, (((0,), (0,)), ((), ())), preferred_element_type=F32)
        hole = (wide >= o) & (wide < o + 8)
        dr[...] = jnp.where(hole, 0.0, dr[...]) - upd[:, :128]
        di[...] = jnp.where(hole, 0.0, di[...]) - upd[:, 128:]
        dr[o:o+8, :] = xr
        di[o:o+8, :] = xi


def beam_kernel(cube, gates, looks, out, got, send, even, odd, raw, spec, rows, part_d, part_r, share_d, share_r,
                sum_d, sum_r, full, look, steer, dr, di, row, w, x_ref, weights,
                own_sem, a_send, a_recv, b_send, b_recv, x_send, x_recv, rd_send, rd_recv, rr_send, rr_recv,
                gd_send, gd_recv, gr_send, gr_recv, w_send, w_recv):
    dop = lax.axis_index("dop")
    rng = lax.axis_index("rng")
    x, z = rng // NZ, lax.rem(rng, NZ)
    root = jnp.where(lax.rem(dop, 2) == 0, ROOTS[0], ROOTS[1])
    is_root = rng == root

    def dop_peer(step):
        return {"dop": lax.rem(dop + step, DOP)}

    def x_peer(step):
        return {"rng": lax.rem(x + step, NX) * NZ + z}

    def z_peer(step):
        return {"rng": x * NZ + lax.rem(z + step, NZ)}

    def loop(count, body, start=1):
        def one(step, carry):
            body(step)
            return carry
        lax.fori_loop(start, count, one, 0)

    def far_first(count, body):
        def one(k):
            j = count - k
            body(jnp.where(lax.rem(j, 2) == 1, (j + 1) // 2, count - j // 2))
        loop(count, one)

    def others(body):
        def one(r):
            @pl.when(r != rng)
            def _():
                body(r)
        loop(RNG, one, 0)

    barrier = pltpu.get_barrier_semaphore()

    def greet(peer):
        pl.semaphore_signal(barrier, inc=1, device_id=peer, device_id_type=MESH)

    loop(DOP, lambda step: greet(dop_peer(step)))
    loop(RNG, lambda step: greet({"rng": lax.rem(rng + step, RNG)}))
    pl.semaphore_wait(barrier, DOP + RNG - 2)

    def tile_of(index):
        return (pl.ds(pl.multiple_of(index // 4 * 16, 16), 16),
                pl.ds(pl.multiple_of(lax.rem(index, 4) * 128, 128), 128))

    def a_copy(step):
        g, c = tile_of(lax.rem(dop + step, DOP))
        return pltpu.make_async_remote_copy(
            src_ref=cube.at[:, :, g, c], dst_ref=got.at[step], send_sem=a_send.at[step],
            recv_sem=a_recv.at[step], device_id=dop_peer(step), device_id_type=MESH)

    far_first(DOP, lambda step: a_copy(step).start())
    g, c = tile_of(dop)
    own = pltpu.make_async_copy(cube.at[:, :, g, c], got.at[0], own_sem)
    own.start()

    look[...] = jnp.zeros_like(look)
    look[:, 0:BEAMS] = looks[...]
    slope = 2 * look[...] + 1 - NANG
    lanes = lax.broadcasted_iota(jnp.int32, (128, 128), 1)
    for k in range(4):
        channel = lax.broadcasted_iota(jnp.int32, (128, 128), 0) + 128 * k
        turn = (channel * slope) & (2 * NANG - 1)
        phase = turn.astype(F32) * (math.pi / NANG)
        steer[0, 128*k:128*k+128, :] = jnp.where(lanes < BEAMS, jnp.cos(phase), 0.0)
        steer[1, 128*k:128*k+128, :] = jnp.where(lanes < BEAMS, jnp.sin(phase), 0.0)
    gate = lax.broadcasted_iota(jnp.int32, (64, 48), 0)
    mask = jnp.max(jnp.where(gate == gates[...], 1.0, 0.0), axis=1, keepdims=True)

    own.wait()
    sign = jnp.where(lax.rem(dop, 2) == 0, 1.0, -1.0).astype(F32)
    first = got[0].astype(F32)
    even[...] = first
    odd[...] = sign * first

    def fold(step):
        a_copy(step).wait_recv()
        block = got[step].astype(F32)
        flip = jnp.where(lax.rem(step, 2) == 0, sign, -sign)
        even[...] += block
        odd[...] += flip * block

    loop(DOP, fold)

    cosine, sine = twiddles()
    norm = 1.0 / math.sqrt(PULSES)
    for half in range(2):
        rows8 = slice(8 * half, 8 * half + 8)
        for parity, source in enumerate((even, odd)):
            re = [source[0, q, rows8, :] for q in range(8)]
            im = [source[1, q, rows8, :] for q in range(8)]
            for b in range(parity, DOP, 2):
                up = low = None
                for q in range(8):
                    cb, sb = float(cosine[b * q % 16]), float(sine[b * q % 16])
                    for k, v in ((cb, re[q]), (sb, im[q])):
                        if k != 0.0:
                            up = k * v if up is None else up + k * v
                    for k, v in ((-sb, re[q]), (cb, im[q])):
                        if k != 0.0:
                            low = k * v if low is None else low + k * v
                raw[b, 0, rows8, :] = up * norm
                raw[b, 1, rows8, :] = low * norm
    for b in range(DOP):
        send[b] = raw[b].astype(BF16)

    def b_copy(step):
        return pltpu.make_async_remote_copy(
            src_ref=send.at[lax.rem(dop + step, DOP)], dst_ref=spec.at[:, g, c], send_sem=b_send.at[step],
            recv_sem=b_recv.at[step], device_id=dop_peer(step), device_id_type=MESH)

    far_first(DOP, lambda step: b_copy(step).start())
    spec[:, g, c] = send[dop]
    loop(DOP, lambda step: b_copy(step).wait_recv())

    for i in range(2):
        rows[0, i] = (spec[i].astype(F32) * mask).astype(BF16)

    def x_copy(step):
        return pltpu.make_async_remote_copy(
            src_ref=rows.at[0], dst_ref=rows.at[step], send_sem=x_send.at[step],
            recv_sem=x_recv.at[step], device_id=x_peer(step), device_id_type=MESH)

    far_first(NX, lambda step: x_copy(step).start())
    loop(NX, lambda step: x_copy(step).wait_recv())

    def columns(block):
        at = pl.ds(pl.multiple_of(block * SIDE, SIDE), SIDE)
        return (rows[:, 0, :, at].reshape(256, SIDE), rows[:, 1, :, at].reshape(256, SIDE))

    def dot(a, b):
        return lax.dot_general(a, b, (((0,), (0,)), ((), ())), preferred_element_type=F32)

    def power(a, b):
        return dot(a[0], b[0]) + dot(a[1], b[1])

    def cross(a, b):
        return dot(a[0], b[1]) - dot(a[1], b[0])

    def r_copy(part, share, sends, recvs, step):
        return pltpu.make_async_remote_copy(
            src_ref=part.at[lax.rem(z + step, NZ)], dst_ref=share.at[step], send_sem=sends.at[step],
            recv_sem=recvs.at[step], device_id=z_peer(step), device_id_type=MESH)

    rd_copy = functools.partial(r_copy, part_d, share_d, rd_send, rd_recv)
    rr_copy = functools.partial(r_copy, part_r, share_r, rr_send, rr_recv)
    mine = columns(x)
    eye = lax.broadcasted_iota(jnp.int32, (SIDE, SIDE), 0) - lax.broadcasted_iota(jnp.int32, (SIDE, SIDE), 1)
    part_d[...] = jnp.where(eye >= 0, power(mine, mine), cross(mine, mine)).reshape(NZ, 16, SIDE)
    far_first(NZ, lambda step: rd_copy(step).start())
    near, far = lax.rem(x + 1, NX), lax.rem(x + 2, NX)
    low1, high1 = columns(jnp.minimum(x, near)), columns(jnp.maximum(x, near))
    low2, high2 = columns(jnp.minimum(x, far)), columns(jnp.maximum(x, far))
    part_r[:, :, 0:128] = power(low1, high1).reshape(NZ, 16, SIDE)
    part_r[:, :, 128:256] = cross(low1, high1).reshape(NZ, 16, SIDE)
    part_r[:, :, 256:384] = jnp.where(x < 2, power(low2, high2), cross(low2, high2)).reshape(NZ, 16, SIDE)
    far_first(NZ, lambda step: rr_copy(step).start())

    strip = pl.ds(pl.multiple_of(z * 16, 16), 16)

    def strip_of(r, at):
        return full.at[r // NZ, pl.ds(pl.multiple_of(lax.rem(r, NZ) * 16, 16), 16), at]

    def gd_copy(r, target):
        return pltpu.make_async_remote_copy(
            src_ref=sum_d, dst_ref=strip_of(r, slice(0, 128)), send_sem=gd_send, recv_sem=gd_recv.at[r],
            device_id={"rng": target}, device_id_type=MESH)

    def gr_copy(r, target):
        return pltpu.make_async_remote_copy(
            src_ref=sum_r, dst_ref=strip_of(r, slice(128, 512)), send_sem=gr_send, recv_sem=gr_recv.at[r],
            device_id={"rng": target}, device_id_type=MESH)

    def total(part, share, copy):
        loop(NZ, lambda step: copy(step).wait_recv())
        value = part[z]
        for step in range(1, NZ):
            value = value + share[step]
        return value * (1.0 / TRAIN)

    value_d = total(part_d, share_d, rd_copy)

    @pl.when(jnp.logical_not(is_root))
    def _():
        sum_d[...] = value_d
        gd_copy(rng, root).start()
        sum_r[...] = total(part_r, share_r, rr_copy)
        gr_copy(rng, root).start()

    def w_copy(r):
        return pltpu.make_async_remote_copy(
            src_ref=weights, dst_ref=weights, send_sem=w_send.at[r], recv_sem=w_recv,
            device_id={"rng": r}, device_id_type=MESH)

    @pl.when(is_root)
    def _():
        full[x, strip, 0:128] = value_d
        others(lambda r: gd_copy(r, root).wait_recv())
        trace = jnp.zeros((), F32)
        for i in range(4):
            trace = trace + jnp.sum(jnp.where(eye == 0, full[i, :, 0:128], 0.0))
        load = LOAD * trace / 512.0
        for i in range(4):
            t = full[i, :, 0:128]
            tt = t.T
            row[i, 0:128, 128*i:128*i+128] = jnp.where(eye > 0, t, tt) + jnp.where(eye == 0, load, 0.0)
            row[i, 128:256, 128*i:128*i+128] = jnp.where(eye > 0, tt, jnp.where(eye < 0, -t, 0.0))
            row[i, 0:128, 512:640] = steer[0, 128*i:128*i+128, :]
            row[i, 128:256, 512:640] = steer[1, 128*i:128*i+128, :]

        def rest():
            full[x, strip, 128:512] = total(part_r, share_r, rr_copy)
            others(lambda r: gr_copy(r, root).wait_recv())
            for i in range(4):
                for j in range(i + 1, 4):
                    (a, b), (e, d) = place(i, j)
                    row[i, 0:128, 128*j:128*j+128] = full[a, :, 128*b:128*b+128]
                    row[i, 128:256, 128*j:128*j+128] = -full[e, :, 128*d:128*d+128]

        solve(rest, steer, row, w, x_ref, dr, di, weights)
        others(lambda r: w_copy(r).start())

    @pl.when(jnp.logical_not(is_root))
    def _():
        w_copy(root).wait_recv()

    across = (((1,), (1,)), ((), ()))
    with_re = lax.dot_general(weights[...], spec[0], across, preferred_element_type=F32)
    with_im = lax.dot_general(weights[...], spec[1], across, preferred_element_type=F32)
    out[0] = with_re[0:8] + with_im[8:16]
    out[1] = with_re[8:16] - with_im[0:8]

    @pl.when(is_root)
    def _():
        others(lambda r: w_copy(r).wait_send())

    @pl.when(jnp.logical_not(is_root))
    def _():
        gd_copy(rng, root).wait_send()
        gr_copy(rng, root).wait_send()

    loop(DOP, lambda step: a_copy(step).wait_send())
    loop(DOP, lambda step: b_copy(step).wait_send())
    loop(NX, lambda step: x_copy(step).wait_send())
    loop(NZ, lambda step: rd_copy(step).wait_send())
    loop(NZ, lambda step: rr_copy(step).wait_send())


def place(i, j):
    if j - i == 1:
        return (i, 1), (i, 2)
    if j - i == 3:
        return (3, 1), (3, 2)
    return (i, 3), (i + 2, 3)


def solve(rest, steer, row, w, x, dr, di, weights):
    def body(k, carry):
        for kk in range(4):
            @pl.when(k == kk)
            def _():
                dr[...] = row[kk, 0:128, 128*kk:128*kk+128]
                di[...] = row[kk, 128:256, 128*kk:128*kk+128]
        invert_block(dr, di)
        for kk in range(4):
            @pl.when(k == kk)
            def _():
                if kk == 0:
                    rest()
                s = 128 * (kk + 1)
                a, b = dr[...], di[...]
                emb = jnp.concatenate([jnp.concatenate([a, -b], 1), jnp.concatenate([b, a], 1)], 0)
                w[kk, :, s:640] = jnp.dot(emb, row[kk, :, s:640], preferred_element_type=F32, precision=HIGH)
                for i in range(kk + 1, 4):
                    c = 128 * i
                    lhs = row[kk, :, c:c+128]
                    wr = w[kk, 0:128, c:640]
                    wi = w[kk, 128:256, c:640]
                    both = jnp.concatenate([jnp.concatenate([wr, wi], 1), jnp.concatenate([wi, -wr], 1)], 0)
                    n = 640 - c
                    u = lax.dot_general(lhs, both, (((0,), (0,)), ((), ())), preferred_element_type=F32, precision=HIGH)
                    row[i, 0:128, c:640] -= u[:, :n]
                    row[i, 128:256, c:640] -= u[:, n:]
        return carry

    lax.fori_loop(0, 4, body, 0)
    q = jnp.zeros((1, 128), F32)
    for k in (3, 2, 1, 0):
        y = w[k, :, 512:640]
        for j in range(k + 1, 4):
            wr = w[k, 0:128, 128*j:128*j+128]
            wi = w[k, 128:256, 128*j:128*j+128]
            emb = jnp.concatenate([jnp.concatenate([wr, -wi], 1), jnp.concatenate([wi, wr], 1)], 0)
            y = y - jnp.dot(emb, x[j], preferred_element_type=F32, precision=HIGH)
        x[k] = y
        for h in range(2):
            q = q + jnp.sum(y[128*h:128*h+128] * steer[h, 128*k:128*k+128, :], axis=0, keepdims=True)
    lanes = lax.broadcasted_iota(jnp.int32, (1, 128), 1)
    scale = lax.rsqrt(jnp.where(lanes < BEAMS, q, 1.0))
    for k in range(4):
        both = [(x[k, 128*h:128*h+128] * scale).T[0:8] for h in range(2)]
        weights[:, 128*k:128*k+128] = jnp.concatenate(both, 0).astype(BF16)


def beams(cube, gates, looks):
    dma = pltpu.SemaphoreType.DMA
    return pl.pallas_call(
        beam_kernel,
        out_shape=jax.ShapeDtypeStruct((2, BEAMS, 64), F32),
        in_specs=[pl.BlockSpec(memory_space=pl.ANY), pl.BlockSpec(memory_space=pltpu.VMEM),
                  pl.BlockSpec(memory_space=pltpu.VMEM)],
        out_specs=pl.BlockSpec(memory_space=pltpu.VMEM),
        scratch_shapes=[
            pltpu.VMEM((DOP, 2, 8, 16, 128), BF16),
            pltpu.VMEM((DOP, 2, 16, 128), BF16),
            pltpu.VMEM((2, 8, 16, 128), F32),
            pltpu.VMEM((2, 8, 16, 128), F32),
            pltpu.VMEM((DOP, 2, 16, 128), F32),
            pltpu.VMEM((2, 64, 512), BF16),
            pltpu.VMEM((NX, 2, 64, 512), BF16),
            pltpu.VMEM((NZ, 16, 128), F32),
            pltpu.VMEM((NZ, 16, 384), F32),
            pltpu.VMEM((NZ, 16, 128), F32),
            pltpu.VMEM((NZ, 16, 384), F32),
            pltpu.VMEM((16, 128), F32),
            pltpu.VMEM((16, 384), F32),
            pltpu.VMEM((4, SIDE, 512), F32),
            pltpu.VMEM((1, 128), jnp.int32),
            pltpu.VMEM((2, 512, 128), F32),
            pltpu.VMEM((128, 128), F32),
            pltpu.VMEM((128, 128), F32),
            pltpu.VMEM((4, 256, 640), F32),
            pltpu.VMEM((4, 256, 640), F32),
            pltpu.VMEM((4, 256, 128), F32),
            pltpu.VMEM((16, 512), BF16),
            dma(()),
            dma((DOP,)), dma((DOP,)), dma((DOP,)), dma((DOP,)), dma((NX,)), dma((NX,)),
            dma((NZ,)), dma((NZ,)), dma((NZ,)), dma((NZ,)),
            dma(()), dma((RNG,)), dma(()), dma((RNG,)), dma((RNG,)), dma(()),
        ],
        compiler_params=pltpu.CompilerParams(collective_id=0, has_side_effects=True, vmem_limit_bytes=48 << 20),
        cost_estimate=pl.CostEstimate(flops=10**9, bytes_accessed=10**7, transcendentals=0),
    )(cube, gates, looks)


def on_device(radar_cube, train_gates, look_angles):
    return beams(radar_cube, train_gates, look_angles)[:, None]


def solution(mesh):
    return jax.shard_map(
        on_device,
        mesh=mesh,
        in_specs=(P(None, "dop", "rng", None), P("dop", "rng"), P("dop", None)),
        out_specs=P(None, "dop", None, "rng"),
        check_vma=False,
    )
```

```python
import functools
import math

import jax
import jax.numpy as jnp
import numpy as np
from jax import lax
from jax.experimental import pallas as pl
from jax.experimental.pallas import tpu as pltpu
from jax.sharding import PartitionSpec as P

F32 = jnp.float32
BF16 = jnp.bfloat16
HIGH = lax.Precision.HIGHEST
MESH = pl.DeviceIdType.MESH
PULSES = 128
NANG = 256
BEAMS = 8
LOAD = 1e-05
DOP = 16
NX = 4
NZ = 8
RNG = NX * NZ
SIDE = 128
TR = 48
TRAIN = 1536
ROOTS = (0, 20)


def twiddles():
    angle = 2.0 * math.pi * np.arange(16) / 16
    rounded = lambda v: np.round(v, 12).astype(BF16).astype(np.float32)
    return rounded(np.cos(angle)), rounded(np.sin(angle))


def parts3(x):
    a = x.astype(BF16).astype(F32)
    r = x - a
    b = r.astype(BF16).astype(F32)
    c = (r - b).astype(BF16).astype(F32)
    return a, b, c

def left6(t):
    a, b, c = t
    return [a, a, b, a, b, c]

def right6(t):
    a, b, c = t
    return [a, b, a, c, b, a]

def neg(t):
    return tuple(-v for v in t)

def invert_block(dr, di):
    lane = lax.broadcasted_iota(jnp.int32, (8, 128), 1)
    sub = lax.broadcasted_iota(jnp.int32, (8, 128), 0)
    wide = lax.broadcasted_iota(jnp.int32, (128, 128), 1)

    def spread(v, o):
        return [jnp.broadcast_to(v[:, o+j:o+j+1], (8, 128)) for j in range(8)]

    rr, ri = dr[0:8, :], di[0:8, :]
    for p in range(16):
        o = 8 * p
        cr, ci = spread(rr, o), spread(ri, o)
        inside = (lane >= o) & (lane < o + 8)
        xr = jnp.where(inside, jnp.where(lane == o + sub, 1.0, 0.0), rr)
        xi = jnp.where(inside, 0.0, ri)
        for i in range(8):
            inv = 1.0 / cr[i][i:i+1, :]
            here = sub == i

            def step(vr, vi):
                tr = vr[i:i+1, :] * inv
                ti = vi[i:i+1, :] * inv
                nr = jnp.where(here, tr, vr - (cr[i] * tr - ci[i] * ti))
                ni = jnp.where(here, ti, vi - (cr[i] * ti + ci[i] * tr))
                return nr, ni

            for j in range(i + 1, 8):
                cr[j], ci[j] = step(cr[j], ci[j])
            xr, xi = step(xr, xi)
        if p < 15:
            br, bi = dr[o+8:o+16, :], di[o+8:o+16, :]
            er, ei = spread(br, o), spread(bi, o)
            ar, ai = [], []
            for j in range(8):
                tr, ti = xr[j:j+1, :], xi[j:j+1, :]
                ar.append(er[j] * tr - ei[j] * ti)
                ai.append(er[j] * ti + ei[j] * tr)
            while len(ar) > 1:
                ar = [a + b for a, b in zip(ar[::2], ar[1::2])]
                ai = [a + b for a, b in zip(ai[::2], ai[1::2])]
            ahead_r = jnp.where(inside, 0.0, br) - ar[0]
            ahead_i = jnp.where(inside, 0.0, bi) - ai[0]
        sign = jnp.where(lane < o, -1.0, 1.0)
        a, b = parts3(sign * rr), parts3(-sign * ri)
        left = jnp.concatenate(left6(a) + left6(b), 0).astype(BF16)
        u, v = parts3(xr), parts3(xi)
        right = jnp.concatenate([
            jnp.concatenate(right6(u) + right6(neg(v)), 0),
            jnp.concatenate(right6(v) + right6(u), 0)], 1).astype(BF16)
        upd = lax.dot_general(left, right, (((0,), (0,)), ((), ())), preferred_element_type=F32)
        hole = (wide >= o) & (wide < o + 8)
        dr[...] = jnp.where(hole, 0.0, dr[...]) - upd[:, :128]
        di[...] = jnp.where(hole, 0.0, di[...]) - upd[:, 128:]
        dr[o:o+8, :] = xr
        di[o:o+8, :] = xi
        if p < 15:
            rr, ri = ahead_r, ahead_i


def beam_kernel(cube, indices, out, got, send, even, odd, raw, spec, rows, part_d, part_r, share_d, share_r,
                sum_d, sum_r, full, steer, dr, di, row, w, x_ref, weights,
                own_sem, a_send, a_recv, b_send, b_recv, x_send, x_recv, rd_send, rd_recv, rr_send, rr_recv,
                gd_send, gd_recv, gr_send, gr_recv, w_send, w_recv):
    dop = lax.axis_index("dop")
    rng = lax.axis_index("rng")
    x, z = rng // NZ, lax.rem(rng, NZ)
    root = jnp.where(lax.rem(dop, 2) == 0, ROOTS[0], ROOTS[1])
    is_root = rng == root

    def dop_peer(step):
        return {"dop": lax.rem(dop + step, DOP)}

    def x_peer(step):
        return {"rng": lax.rem(x + step, NX) * NZ + z}

    def z_peer(step):
        return {"rng": x * NZ + lax.rem(z + step, NZ)}

    def loop(count, body, start=1):
        def one(step, carry):
            body(step)
            return carry
        lax.fori_loop(start, count, one, 0)

    def far_first(count, body):
        def one(k):
            j = count - k
            body(jnp.where(lax.rem(j, 2) == 1, (j + 1) // 2, count - j // 2))
        loop(count, one)

    def others(body):
        def one(r):
            @pl.when(r != rng)
            def _():
                body(r)
        loop(RNG, one, 0)

    barrier = pltpu.get_barrier_semaphore()

    def greet(peer):
        pl.semaphore_signal(barrier, inc=1, device_id=peer, device_id_type=MESH)

    loop(DOP, lambda step: greet(dop_peer(step)))
    aside = (root // NZ != x) & (lax.rem(root, NZ) != z)

    @pl.when(is_root)
    def _():
        loop(RNG, lambda step: greet({"rng": lax.rem(rng + step, RNG)}))

    @pl.when(jnp.logical_not(is_root))
    def _():
        loop(NX, lambda step: greet(x_peer(step)))
        loop(NZ, lambda step: greet(z_peer(step)))

    @pl.when(aside)
    def _():
        greet({"rng": root})

    near_count = DOP + NX + NZ - 3
    pl.semaphore_wait(barrier, jnp.where(is_root, DOP + RNG - 2, jnp.where(aside, near_count + 1, near_count)))

    def tile_of(index):
        return (pl.ds(pl.multiple_of(index // 4 * 16, 16), 16),
                pl.ds(pl.multiple_of(lax.rem(index, 4) * 128, 128), 128))

    def a_copy(step):
        g, c = tile_of(lax.rem(dop + step, DOP))
        return pltpu.make_async_remote_copy(
            src_ref=cube.at[:, :, g, c], dst_ref=got.at[step], send_sem=a_send.at[step],
            recv_sem=a_recv.at[step], device_id=dop_peer(step), device_id_type=MESH)

    far_first(DOP, lambda step: a_copy(step).start())
    g, c = tile_of(dop)
    own = pltpu.make_async_copy(cube.at[:, :, g, c], got.at[0], own_sem)
    own.start()

    slope = 2 * indices[1:2] + 1 - NANG
    lanes = lax.broadcasted_iota(jnp.int32, (128, 128), 1)
    for k in range(4):
        channel = lax.broadcasted_iota(jnp.int32, (128, 128), 0) + 128 * k
        turn = (channel * slope) & (2 * NANG - 1)
        phase = turn.astype(F32) * (math.pi / NANG)
        steer[0, 128*k:128*k+128, :] = jnp.where(lanes < BEAMS, jnp.cos(phase), 0.0)
        steer[1, 128*k:128*k+128, :] = jnp.where(lanes < BEAMS, jnp.sin(phase), 0.0)
    gate = lax.broadcasted_iota(jnp.int32, (64, TR), 0)
    pick = jnp.where(gate == indices[0:1, 0:TR], 1.0, 0.0).astype(BF16)

    own.wait()
    sign = jnp.where(lax.rem(dop, 2) == 0, 1.0, -1.0).astype(F32)
    first = got[0].astype(F32)
    even[...] = first
    odd[...] = sign * first

    def fold(step):
        a_copy(step).wait_recv()
        block = got[step].astype(F32)
        flip = jnp.where(lax.rem(step, 2) == 0, sign, -sign)
        even[...] += block
        odd[...] += flip * block

    loop(DOP, fold)

    cosine, sine = twiddles()
    norm = 1.0 / math.sqrt(PULSES)
    for half in range(2):
        rows8 = slice(8 * half, 8 * half + 8)
        for parity, source in enumerate((even, odd)):
            re = [source[0, q, rows8, :] for q in range(8)]
            im = [source[1, q, rows8, :] for q in range(8)]
            for b in range(parity, DOP, 2):
                up = low = None
                for q in range(8):
                    cb, sb = float(cosine[b * q % 16]), float(sine[b * q % 16])
                    for k, v in ((cb, re[q]), (sb, im[q])):
                        if k != 0.0:
                            up = k * v if up is None else up + k * v
                    for k, v in ((-sb, re[q]), (cb, im[q])):
                        if k != 0.0:
                            low = k * v if low is None else low + k * v
                raw[b, 0, rows8, :] = up * norm
                raw[b, 1, rows8, :] = low * norm
    for b in range(DOP):
        send[b] = raw[b].astype(BF16)

    def b_copy(step):
        return pltpu.make_async_remote_copy(
            src_ref=send.at[lax.rem(dop + step, DOP)], dst_ref=spec.at[:, g, c], send_sem=b_send.at[step],
            recv_sem=b_recv.at[step], device_id=dop_peer(step), device_id_type=MESH)

    far_first(DOP, lambda step: b_copy(step).start())
    spec[:, g, c] = send[dop]
    loop(DOP, lambda step: b_copy(step).wait_recv())

    for i in range(2):
        rows[0, i] = lax.dot_general(
            pick, spec[i], (((0,), (0,)), ((), ())), preferred_element_type=F32).astype(BF16)

    def x_copy(step):
        return pltpu.make_async_remote_copy(
            src_ref=rows.at[0], dst_ref=rows.at[step], send_sem=x_send.at[step],
            recv_sem=x_recv.at[step], device_id=x_peer(step), device_id_type=MESH)

    far_first(NX, lambda step: x_copy(step).start())
    loop(NX, lambda step: x_copy(step).wait_recv())

    def columns(block):
        at = pl.ds(pl.multiple_of(block * SIDE, SIDE), SIDE)
        return (rows[:, 0, :, at].reshape(NX * TR, SIDE), rows[:, 1, :, at].reshape(NX * TR, SIDE))

    def dot(a, b):
        return lax.dot_general(a, b, (((0,), (0,)), ((), ())), preferred_element_type=F32)

    def power(a, b):
        return dot(a[0], b[0]) + dot(a[1], b[1])

    def cross(a, b):
        return dot(a[0], b[1]) - dot(a[1], b[0])

    def r_copy(part, share, sends, recvs, step):
        return pltpu.make_async_remote_copy(
            src_ref=part.at[lax.rem(z + step, NZ)], dst_ref=share.at[step], send_sem=sends.at[step],
            recv_sem=recvs.at[step], device_id=z_peer(step), device_id_type=MESH)

    rd_copy = functools.partial(r_copy, part_d, share_d, rd_send, rd_recv)
    rr_copy = functools.partial(r_copy, part_r, share_r, rr_send, rr_recv)
    mine = columns(x)
    eye = lax.broadcasted_iota(jnp.int32, (SIDE, SIDE), 0) - lax.broadcasted_iota(jnp.int32, (SIDE, SIDE), 1)
    part_d[...] = jnp.where(eye >= 0, power(mine, mine), cross(mine, mine)).reshape(NZ, 16, SIDE)
    far_first(NZ, lambda step: rd_copy(step).start())
    near, far = lax.rem(x + 1, NX), lax.rem(x + 2, NX)
    low1, high1 = columns(jnp.minimum(x, near)), columns(jnp.maximum(x, near))
    low2, high2 = columns(jnp.minimum(x, far)), columns(jnp.maximum(x, far))
    part_r[:, :, 0:128] = power(low1, high1).reshape(NZ, 16, SIDE)
    part_r[:, :, 128:256] = cross(low1, high1).reshape(NZ, 16, SIDE)
    part_r[:, :, 256:384] = jnp.where(x < 2, power(low2, high2), cross(low2, high2)).reshape(NZ, 16, SIDE)
    far_first(NZ, lambda step: rr_copy(step).start())

    strip = pl.ds(pl.multiple_of(z * 16, 16), 16)

    def strip_of(r, at):
        return full.at[r // NZ, pl.ds(pl.multiple_of(lax.rem(r, NZ) * 16, 16), 16), at]

    def gd_copy(r, target):
        return pltpu.make_async_remote_copy(
            src_ref=sum_d, dst_ref=strip_of(r, slice(0, 128)), send_sem=gd_send, recv_sem=gd_recv.at[r],
            device_id={"rng": target}, device_id_type=MESH)

    def gr_copy(r, target):
        return pltpu.make_async_remote_copy(
            src_ref=sum_r, dst_ref=strip_of(r, slice(128, 512)), send_sem=gr_send, recv_sem=gr_recv.at[r],
            device_id={"rng": target}, device_id_type=MESH)

    def total(part, share, copy):
        loop(NZ, lambda step: copy(step).wait_recv())
        value = part[z]
        for step in range(1, NZ):
            value = value + share[step]
        return value * (1.0 / TRAIN)

    value_d = total(part_d, share_d, rd_copy)

    @pl.when(jnp.logical_not(is_root))
    def _():
        sum_d[...] = value_d
        gd_copy(rng, root).start()
        sum_r[...] = total(part_r, share_r, rr_copy)
        gr_copy(rng, root).start()

    def w_copy(r):
        return pltpu.make_async_remote_copy(
            src_ref=weights, dst_ref=weights, send_sem=w_send.at[r], recv_sem=w_recv,
            device_id={"rng": r}, device_id_type=MESH)

    @pl.when(is_root)
    def _():
        full[x, strip, 0:128] = value_d
        others(lambda r: gd_copy(r, root).wait_recv())
        trace = jnp.zeros((), F32)
        for i in range(4):
            trace = trace + jnp.sum(jnp.where(eye == 0, full[i, :, 0:128], 0.0))
        load = LOAD * trace / 512.0
        for i in range(4):
            t = full[i, :, 0:128]
            tt = t.T
            row[i, 0:128, 128*i:128*i+128] = jnp.where(eye > 0, t, tt) + jnp.where(eye == 0, load, 0.0)
            row[i, 128:256, 128*i:128*i+128] = jnp.where(eye > 0, tt, jnp.where(eye < 0, -t, 0.0))
            row[i, 0:128, 512:640] = steer[0, 128*i:128*i+128, :]
            row[i, 128:256, 512:640] = steer[1, 128*i:128*i+128, :]

        def rest():
            full[x, strip, 128:512] = total(part_r, share_r, rr_copy)
            others(lambda r: gr_copy(r, root).wait_recv())
            for i in range(4):
                for j in range(i + 1, 4):
                    (a, b), (e, d) = place(i, j)
                    row[i, 0:128, 128*j:128*j+128] = full[a, :, 128*b:128*b+128]
                    row[i, 128:256, 128*j:128*j+128] = -full[e, :, 128*d:128*d+128]

        solve(rest, steer, row, w, x_ref, dr, di, weights)
        others(lambda r: w_copy(r).start())

    @pl.when(jnp.logical_not(is_root))
    def _():
        w_copy(root).wait_recv()

    across = (((1,), (1,)), ((), ()))
    with_re = lax.dot_general(weights[...], spec[0], across, preferred_element_type=F32)
    with_im = lax.dot_general(weights[...], spec[1], across, preferred_element_type=F32)
    out[0] = with_re[0:8] + with_im[8:16]
    out[1] = with_re[8:16] - with_im[0:8]

    @pl.when(is_root)
    def _():
        others(lambda r: w_copy(r).wait_send())

    @pl.when(jnp.logical_not(is_root))
    def _():
        gd_copy(rng, root).wait_send()
        gr_copy(rng, root).wait_send()

    loop(DOP, lambda step: a_copy(step).wait_send())
    loop(DOP, lambda step: b_copy(step).wait_send())
    loop(NX, lambda step: x_copy(step).wait_send())
    loop(NZ, lambda step: rd_copy(step).wait_send())
    loop(NZ, lambda step: rr_copy(step).wait_send())


def place(i, j):
    if j - i == 1:
        return (i, 1), (i, 2)
    if j - i == 3:
        return (3, 1), (3, 2)
    return (i, 3), (i + 2, 3)


def solve(rest, steer, row, w, x, dr, di, weights):
    def body(k, carry):
        for kk in range(4):
            @pl.when(k == kk)
            def _():
                dr[...] = row[kk, 0:128, 128*kk:128*kk+128]
                di[...] = row[kk, 128:256, 128*kk:128*kk+128]
        invert_block(dr, di)
        for kk in range(4):
            @pl.when(k == kk)
            def _():
                if kk == 0:
                    rest()
                s = 128 * (kk + 1)
                a, b = dr[...], di[...]
                emb = jnp.concatenate([jnp.concatenate([a, -b], 1), jnp.concatenate([b, a], 1)], 0)
                w[kk, :, s:640] = jnp.dot(emb, row[kk, :, s:640], preferred_element_type=F32, precision=HIGH)
                for i in range(kk + 1, 4):
                    c = 128 * i
                    lhs = row[kk, :, c:c+128]
                    wr = w[kk, 0:128, c:640]
                    wi = w[kk, 128:256, c:640]
                    both = jnp.concatenate([jnp.concatenate([wr, wi], 1), jnp.concatenate([wi, -wr], 1)], 0)
                    n = 640 - c
                    u = lax.dot_general(lhs, both, (((0,), (0,)), ((), ())), preferred_element_type=F32, precision=HIGH)
                    row[i, 0:128, c:640] -= u[:, :n]
                    row[i, 128:256, c:640] -= u[:, n:]
        return carry

    lax.fori_loop(0, 4, body, 0)
    q = jnp.zeros((1, 128), F32)
    for k in (3, 2, 1, 0):
        y = w[k, :, 512:640]
        for j in range(k + 1, 4):
            wr = w[k, 0:128, 128*j:128*j+128]
            wi = w[k, 128:256, 128*j:128*j+128]
            emb = jnp.concatenate([jnp.concatenate([wr, -wi], 1), jnp.concatenate([wi, wr], 1)], 0)
            y = y - jnp.dot(emb, x[j], preferred_element_type=F32, precision=HIGH)
        x[k] = y
        for h in range(2):
            q = q + jnp.sum(y[128*h:128*h+128] * steer[h, 128*k:128*k+128, :], axis=0, keepdims=True)
    lanes = lax.broadcasted_iota(jnp.int32, (1, 128), 1)
    scale = lax.rsqrt(jnp.where(lanes < BEAMS, q, 1.0))
    for k in range(4):
        both = [(x[k, 128*h:128*h+128] * scale).T[0:8] for h in range(2)]
        weights[:, 128*k:128*k+128] = jnp.concatenate(both, 0).astype(BF16)


def beams(cube, indices):
    dma = pltpu.SemaphoreType.DMA
    return pl.pallas_call(
        beam_kernel,
        out_shape=jax.ShapeDtypeStruct((2, BEAMS, 64), F32),
        in_specs=[pl.BlockSpec(memory_space=pl.ANY), pl.BlockSpec(memory_space=pltpu.VMEM)],
        out_specs=pl.BlockSpec(memory_space=pltpu.VMEM),
        scratch_shapes=[
            pltpu.VMEM((DOP, 2, 8, 16, 128), BF16),
            pltpu.VMEM((DOP, 2, 16, 128), BF16),
            pltpu.VMEM((2, 8, 16, 128), F32),
            pltpu.VMEM((2, 8, 16, 128), F32),
            pltpu.VMEM((DOP, 2, 16, 128), F32),
            pltpu.VMEM((2, 64, 512), BF16),
            pltpu.VMEM((NX, 2, TR, 512), BF16),
            pltpu.VMEM((NZ, 16, 128), F32),
            pltpu.VMEM((NZ, 16, 384), F32),
            pltpu.VMEM((NZ, 16, 128), F32),
            pltpu.VMEM((NZ, 16, 384), F32),
            pltpu.VMEM((16, 128), F32),
            pltpu.VMEM((16, 384), F32),
            pltpu.VMEM((4, SIDE, 512), F32),
            pltpu.VMEM((2, 512, 128), F32),
            pltpu.VMEM((128, 128), F32),
            pltpu.VMEM((128, 128), F32),
            pltpu.VMEM((4, 256, 640), F32),
            pltpu.VMEM((4, 256, 640), F32),
            pltpu.VMEM((4, 256, 128), F32),
            pltpu.VMEM((16, 512), BF16),
            dma(()),
            dma((DOP,)), dma((DOP,)), dma((DOP,)), dma((DOP,)), dma((NX,)), dma((NX,)),
            dma((NZ,)), dma((NZ,)), dma((NZ,)), dma((NZ,)),
            dma(()), dma((RNG,)), dma(()), dma((RNG,)), dma((RNG,)), dma(()),
        ],
        compiler_params=pltpu.CompilerParams(collective_id=0, has_side_effects=True, vmem_limit_bytes=62 << 20),
        cost_estimate=pl.CostEstimate(flops=10**9, bytes_accessed=10**7, transcendentals=0),
    )(cube, indices)


def on_device(radar_cube, train_gates, look_angles):
    indices = jnp.concatenate([
        jnp.pad(train_gates, ((0, 0), (0, 128 - TR))), jnp.pad(look_angles, ((0, 0), (0, 128 - BEAMS)))], 0)
    return beams(radar_cube, indices)[:, None]


def solution(mesh):
    return jax.shard_map(
        on_device,
        mesh=mesh,
        in_specs=(P(None, "dop", "rng", None), P("dop", "rng"), P("dop", None)),
        out_specs=P(None, "dop", None, "rng"),
        check_vma=False,
    )
```

```python
import functools
import math

import jax
import jax.numpy as jnp
import numpy as np
from jax import lax
from jax.experimental import pallas as pl
from jax.experimental.pallas import tpu as pltpu
from jax.sharding import PartitionSpec as P

F32 = jnp.float32
BF16 = jnp.bfloat16
HIGH = lax.Precision.HIGHEST
MESH = pl.DeviceIdType.MESH
PULSES = 128
NANG = 256
BEAMS = 8
LOAD = 1e-05
DOP = 16
NX = 4
NZ = 8
RNG = NX * NZ
TR = 48
TRAIN = 1536
ROOTS = (0, 20)


def twiddles():
    angle = 2.0 * math.pi * np.arange(16) / 16
    rounded = lambda v: np.round(v, 12).astype(BF16).astype(np.float32)
    return rounded(np.cos(angle)), rounded(np.sin(angle))


def parts3(x):
    a = x.astype(BF16).astype(F32)
    r = x - a
    b = r.astype(BF16).astype(F32)
    c = (r - b).astype(BF16).astype(F32)
    return a, b, c

def left6(t):
    a, b, c = t
    return [a, a, b, a, b, c]

def right6(t):
    a, b, c = t
    return [a, b, a, c, b, a]

def neg(t):
    return tuple(-v for v in t)

def invert_block(dr, di):
    lane = lax.broadcasted_iota(jnp.int32, (8, 128), 1)
    sub = lax.broadcasted_iota(jnp.int32, (8, 128), 0)
    wide = lax.broadcasted_iota(jnp.int32, (128, 128), 1)

    def spread(v, o):
        return [jnp.broadcast_to(v[:, o+j:o+j+1], (8, 128)) for j in range(8)]

    rr, ri = dr[0:8, :], di[0:8, :]
    for p in range(16):
        o = 8 * p
        cr, ci = spread(rr, o), spread(ri, o)
        inside = (lane >= o) & (lane < o + 8)
        xr = jnp.where(inside, jnp.where(lane == o + sub, 1.0, 0.0), rr)
        xi = jnp.where(inside, 0.0, ri)
        for i in range(8):
            inv = 1.0 / cr[i][i:i+1, :]
            here = sub == i

            def step(vr, vi):
                tr = vr[i:i+1, :] * inv
                ti = vi[i:i+1, :] * inv
                nr = jnp.where(here, tr, vr - (cr[i] * tr - ci[i] * ti))
                ni = jnp.where(here, ti, vi - (cr[i] * ti + ci[i] * tr))
                return nr, ni

            for j in range(i + 1, 8):
                cr[j], ci[j] = step(cr[j], ci[j])
            xr, xi = step(xr, xi)
        if p < 15:
            br, bi = dr[o+8:o+16, :], di[o+8:o+16, :]
            er, ei = spread(br, o), spread(bi, o)
            ar, ai = [], []
            for j in range(8):
                tr, ti = xr[j:j+1, :], xi[j:j+1, :]
                ar.append(er[j] * tr - ei[j] * ti)
                ai.append(er[j] * ti + ei[j] * tr)
            while len(ar) > 1:
                ar = [a + b for a, b in zip(ar[::2], ar[1::2])]
                ai = [a + b for a, b in zip(ai[::2], ai[1::2])]
            ahead_r = jnp.where(inside, 0.0, br) - ar[0]
            ahead_i = jnp.where(inside, 0.0, bi) - ai[0]
        sign = jnp.where(lane < o, -1.0, 1.0)
        a, b = parts3(sign * rr), parts3(-sign * ri)
        left = jnp.concatenate(left6(a) + left6(b), 0).astype(BF16)
        u, v = parts3(xr), parts3(xi)
        right = jnp.concatenate([
            jnp.concatenate(right6(u) + right6(neg(v)), 0),
            jnp.concatenate(right6(v) + right6(u), 0)], 1).astype(BF16)
        upd = lax.dot_general(left, right, (((0,), (0,)), ((), ())), preferred_element_type=F32)
        hole = (wide >= o) & (wide < o + 8)
        dr[...] = jnp.where(hole, 0.0, dr[...]) - upd[:, :128]
        di[...] = jnp.where(hole, 0.0, di[...]) - upd[:, 128:]
        dr[o:o+8, :] = xr
        di[o:o+8, :] = xi
        if p < 15:
            rr, ri = ahead_r, ahead_i


def beam_kernel(cube, indices, out, got, send, even, odd, raw, spec, rows, stat, stats, big, steer, dr, di, row, w,
                emb, s_ref, y_ref, x_ref, weights,
                own_sem, a_send, a_recv, b_send, b_recv, t_send, t_recv, g_send, g_recv, w_send, w_recv):
    dop = lax.axis_index("dop")
    rng = lax.axis_index("rng")
    root = jnp.where(lax.rem(dop, 2) == 0, ROOTS[0], ROOTS[1])
    is_root = rng == root

    def dop_peer(step):
        return {"dop": lax.rem(dop + step, DOP)}

    def loop(count, body, start=1):
        def one(step, carry):
            body(step)
            return carry
        lax.fori_loop(start, count, one, 0)

    def far_first(count, body):
        def one(k):
            j = count - k
            body(jnp.where(lax.rem(j, 2) == 1, (j + 1) // 2, count - j // 2))
        loop(count, one)

    def others(body):
        def one(r):
            @pl.when(r != rng)
            def _():
                body(r)
        loop(RNG, one, 0)

    barrier = pltpu.get_barrier_semaphore()

    def greet(peer):
        pl.semaphore_signal(barrier, inc=1, device_id=peer, device_id_type=MESH)

    loop(DOP, lambda step: greet(dop_peer(step)))

    @pl.when(is_root)
    def _():
        others(lambda r: greet({"rng": r}))

    @pl.when(jnp.logical_not(is_root))
    def _():
        greet({"rng": root})

    pl.semaphore_wait(barrier, jnp.where(is_root, DOP + RNG - 2, DOP))

    def tile_of(index):
        return (pl.ds(pl.multiple_of(index // 4 * 16, 16), 16),
                pl.ds(pl.multiple_of(lax.rem(index, 4) * 128, 128), 128))

    def a_copy(step):
        g, c = tile_of(lax.rem(dop + step, DOP))
        return pltpu.make_async_remote_copy(
            src_ref=cube.at[:, :, g, c], dst_ref=got.at[step], send_sem=a_send.at[step],
            recv_sem=a_recv.at[step], device_id=dop_peer(step), device_id_type=MESH)

    far_first(DOP, lambda step: a_copy(step).start())
    g, c = tile_of(dop)
    own = pltpu.make_async_copy(cube.at[:, :, g, c], got.at[0], own_sem)
    own.start()

    slope = 2 * indices[1:2] + 1 - NANG
    lanes = lax.broadcasted_iota(jnp.int32, (128, 128), 1)
    for k in range(4):
        channel = lax.broadcasted_iota(jnp.int32, (128, 128), 0) + 128 * k
        turn = (channel * slope) & (2 * NANG - 1)
        phase = turn.astype(F32) * (math.pi / NANG)
        steer[0, 128*k:128*k+128, :] = jnp.where(lanes < BEAMS, jnp.cos(phase), 0.0)
        steer[1, 128*k:128*k+128, :] = jnp.where(lanes < BEAMS, jnp.sin(phase), 0.0)
    gate = lax.broadcasted_iota(jnp.int32, (64, TR), 0)
    pick = jnp.where(gate == indices[0:1, 0:TR], 1.0, 0.0).astype(BF16)

    own.wait()
    sign = jnp.where(lax.rem(dop, 2) == 0, 1.0, -1.0).astype(F32)
    first = got[0].astype(F32)
    even[...] = first
    odd[...] = sign * first

    def fold(step):
        a_copy(step).wait_recv()
        block = got[step].astype(F32)
        flip = jnp.where(lax.rem(step, 2) == 0, sign, -sign)
        even[...] += block
        odd[...] += flip * block

    loop(DOP, fold)

    cosine, sine = twiddles()
    norm = 1.0 / math.sqrt(PULSES)
    for half in range(2):
        rows8 = slice(8 * half, 8 * half + 8)
        for parity, source in enumerate((even, odd)):
            re = [source[0, q, rows8, :] for q in range(8)]
            im = [source[1, q, rows8, :] for q in range(8)]
            for b in range(parity, DOP, 2):
                up = low = None
                for q in range(8):
                    cb, sb = float(cosine[b * q % 16]), float(sine[b * q % 16])
                    for k, v in ((cb, re[q]), (sb, im[q])):
                        if k != 0.0:
                            up = k * v if up is None else up + k * v
                    for k, v in ((-sb, re[q]), (cb, im[q])):
                        if k != 0.0:
                            low = k * v if low is None else low + k * v
                raw[b, 0, rows8, :] = up * norm
                raw[b, 1, rows8, :] = low * norm
    for b in range(DOP):
        send[b] = raw[b].astype(BF16)

    def b_copy(step):
        return pltpu.make_async_remote_copy(
            src_ref=send.at[lax.rem(dop + step, DOP)], dst_ref=spec.at[:, g, c], send_sem=b_send.at[step],
            recv_sem=b_recv.at[step], device_id=dop_peer(step), device_id_type=MESH)

    far_first(DOP, lambda step: b_copy(step).start())
    spec[:, g, c] = send[dop]
    loop(DOP, lambda step: b_copy(step).wait_recv())

    squares = jnp.zeros((8, 128), F32)
    for j in range(4):
        for i in range(2):
            chosen = lax.dot_general(
                pick, spec[i, :, 128*j:128*j+128], (((0,), (0,)), ((), ())), preferred_element_type=F32)
            rows[j, :, 128*i:128*i+128] = chosen.astype(BF16)
            for e in range(0, TR, 8):
                squares = squares + chosen[e:e+8] * chosen[e:e+8]
    stat[...] = squares

    def g_copy(j, r, target):
        return pltpu.make_async_remote_copy(
            src_ref=rows.at[j], dst_ref=big.at[j, r], send_sem=g_send.at[j], recv_sem=g_recv.at[j, r],
            device_id={"rng": target}, device_id_type=MESH)

    def t_copy(r, target):
        return pltpu.make_async_remote_copy(
            src_ref=stat, dst_ref=stats.at[r], send_sem=t_send, recv_sem=t_recv.at[r],
            device_id={"rng": target}, device_id_type=MESH)

    @pl.when(jnp.logical_not(is_root))
    def _():
        g_copy(0, rng, root).start()
        t_copy(rng, root).start()
        for j in range(1, 4):
            g_copy(j, rng, root).start()

    def w_copy(r):
        return pltpu.make_async_remote_copy(
            src_ref=weights, dst_ref=weights, send_sem=w_send.at[r], recv_sem=w_recv,
            device_id={"rng": r}, device_id_type=MESH)

    @pl.when(is_root)
    def _():
        stats[rng] = squares
        for j in range(4):
            big[j, rng] = rows[j]
        others(lambda r: t_copy(r, root).wait_recv())
        load = jnp.sum(jnp.sum(stats[...], axis=0)) * (LOAD / (512.0 * TRAIN))
        for k in range(4):
            top, low = steer[0, 128*k:128*k+128, :], steer[1, 128*k:128*k+128, :]
            s_ref[k] = jnp.concatenate([top, low], 0)

        def arrive(j):
            others(lambda r: g_copy(j, r, root).wait_recv())

        solve(arrive, load, big, steer, s_ref, row, w, emb, y_ref, x_ref, dr, di, weights)
        others(lambda r: w_copy(r).start())

    @pl.when(jnp.logical_not(is_root))
    def _():
        w_copy(root).wait_recv()

    across = (((1,), (1,)), ((), ()))
    with_re = lax.dot_general(weights[...], spec[0], across, preferred_element_type=F32)
    with_im = lax.dot_general(weights[...], spec[1], across, preferred_element_type=F32)
    out[0] = with_re[0:8] + with_im[8:16]
    out[1] = with_re[8:16] - with_im[0:8]

    @pl.when(is_root)
    def _():
        others(lambda r: w_copy(r).wait_send())

    @pl.when(jnp.logical_not(is_root))
    def _():
        t_copy(rng, root).wait_send()
        for j in range(4):
            g_copy(j, rng, root).wait_send()

    loop(DOP, lambda step: a_copy(step).wait_send())
    loop(DOP, lambda step: b_copy(step).wait_send())


def companion(v):
    top, low = v[0:128], v[128:256]
    return jnp.concatenate([jnp.concatenate([top, low], 1), jnp.concatenate([low, -top], 1)], 0)


def solve(arrive, load, big, steer, s_ref, row, w, emb, y_ref, x, dr, di, weights):
    diagonal = lax.broadcasted_iota(jnp.int32, (128, 128), 0) == lax.broadcasted_iota(jnp.int32, (128, 128), 1)
    turned = (((0,), (0,)), ((), ()))

    def high(a, b):
        return jnp.dot(a, b, preferred_element_type=F32, precision=HIGH)

    def high_turned(a, b):
        return lax.dot_general(a, b, turned, preferred_element_type=F32, precision=HIGH)

    def at(k):
        return slice(128 * k, 128 * k + 128)

    def column(j):
        arrive(j)
        mine = big[j].reshape(TRAIN, 256)
        for k in range(j + 1):
            g = lax.dot_general(mine, big[k].reshape(TRAIN, 256), turned, preferred_element_type=F32)
            power = (g[0:128, 0:128] + g[128:256, 128:256]) * (1.0 / TRAIN)
            cross = (g[0:128, 128:256] - g[128:256, 0:128]) * (1.0 / TRAIN)
            if k < j:
                row[k, 0:128, at(j)] = power.T
                row[k, 128:256, at(j)] = cross.T
            else:
                dr[...] = jnp.where(diagonal, power + load, power)
                di[...] = -cross
        for k in range(j):
            if k > 0:
                lhs = jnp.concatenate([row[l, :, at(k)] for l in range(k)], 0)
                rhs = jnp.concatenate([companion(w[l, :, at(j)]) for l in range(k)], 0)
                u = high_turned(lhs, rhs)
                row[k, 0:128, at(j)] -= u[:, 0:128]
                row[k, 128:256, at(j)] -= u[:, 128:256]
            w[k, :, at(j)] = high(emb[k], row[k, :, at(j)])
        if j > 0:
            lhs = jnp.concatenate([row[k, :, at(j)] for k in range(j)], 0)
            rhs = jnp.concatenate([
                jnp.concatenate([companion(w[k, :, at(j)]), companion(y_ref[k])], 1) for k in range(j)], 0)
            u = high_turned(lhs, rhs)
            dr[...] -= u[:, 0:128]
            di[...] -= u[:, 128:256]
            s_ref[j, 0:128] -= u[:, 256:384]
            s_ref[j, 128:256] -= u[:, 384:512]

    def body(k, carry):
        for kk in range(4):
            @pl.when(k == kk)
            def _():
                column(kk)
        invert_block(dr, di)
        a, b = dr[...], di[...]
        emb[k] = jnp.concatenate([jnp.concatenate([a, -b], 1), jnp.concatenate([b, a], 1)], 0)
        y_ref[k] = high(emb[k], s_ref[k])
        return carry

    lax.fori_loop(0, 4, body, 0)
    q = jnp.zeros((1, 128), F32)
    for k in (3, 2, 1, 0):
        y = y_ref[k]
        for j in range(k + 1, 4):
            wr = w[k, 0:128, 128*j:128*j+128]
            wi = w[k, 128:256, 128*j:128*j+128]
            full = jnp.concatenate([jnp.concatenate([wr, -wi], 1), jnp.concatenate([wi, wr], 1)], 0)
            y = y - jnp.dot(full, x[j], preferred_element_type=F32, precision=HIGH)
        x[k] = y
        for h in range(2):
            q = q + jnp.sum(y[128*h:128*h+128] * steer[h, 128*k:128*k+128, :], axis=0, keepdims=True)
    lanes = lax.broadcasted_iota(jnp.int32, (1, 128), 1)
    scale = lax.rsqrt(jnp.where(lanes < BEAMS, q, 1.0))
    for k in range(4):
        both = [(x[k, 128*h:128*h+128] * scale).T[0:8] for h in range(2)]
        weights[:, 128*k:128*k+128] = jnp.concatenate(both, 0).astype(BF16)


def beams(cube, indices):
    dma = pltpu.SemaphoreType.DMA
    return pl.pallas_call(
        beam_kernel,
        out_shape=jax.ShapeDtypeStruct((2, BEAMS, 64), F32),
        in_specs=[pl.BlockSpec(memory_space=pl.ANY), pl.BlockSpec(memory_space=pltpu.VMEM)],
        out_specs=pl.BlockSpec(memory_space=pltpu.VMEM),
        scratch_shapes=[
            pltpu.VMEM((DOP, 2, 8, 16, 128), BF16),
            pltpu.VMEM((DOP, 2, 16, 128), BF16),
            pltpu.VMEM((2, 8, 16, 128), F32),
            pltpu.VMEM((2, 8, 16, 128), F32),
            pltpu.VMEM((DOP, 2, 16, 128), F32),
            pltpu.VMEM((2, 64, 512), BF16),
            pltpu.VMEM((4, TR, 256), BF16),
            pltpu.VMEM((8, 128), F32),
            pltpu.VMEM((RNG, 8, 128), F32),
            pltpu.VMEM((4, RNG, TR, 256), BF16),
            pltpu.VMEM((2, 512, 128), F32),
            pltpu.VMEM((128, 128), F32),
            pltpu.VMEM((128, 128), F32),
            pltpu.VMEM((4, 256, 512), F32),
            pltpu.VMEM((4, 256, 512), F32),
            pltpu.VMEM((4, 256, 256), F32),
            pltpu.VMEM((4, 256, 128), F32),
            pltpu.VMEM((4, 256, 128), F32),
            pltpu.VMEM((4, 256, 128), F32),
            pltpu.VMEM((16, 512), BF16),
            dma(()),
            dma((DOP,)), dma((DOP,)), dma((DOP,)), dma((DOP,)),
            dma(()), dma((RNG,)), dma((4,)), dma((4, RNG)), dma((RNG,)), dma(()),
        ],
        compiler_params=pltpu.CompilerParams(collective_id=0, has_side_effects=True, vmem_limit_bytes=53 << 20),
        cost_estimate=pl.CostEstimate(flops=10**9, bytes_accessed=10**7, transcendentals=0),
    )(cube, indices)


def on_device(radar_cube, train_gates, look_angles):
    indices = jnp.concatenate([
        jnp.pad(train_gates, ((0, 0), (0, 128 - TR))), jnp.pad(look_angles, ((0, 0), (0, 128 - BEAMS)))], 0)
    return beams(radar_cube, indices)[:, None]


def solution(mesh):
    return jax.shard_map(
        on_device,
        mesh=mesh,
        in_specs=(P(None, "dop", "rng", None), P("dop", "rng"), P("dop", None)),
        out_specs=P(None, "dop", None, "rng"),
        check_vma=False,
    )
```

```python
import functools
import math

import jax
import jax.numpy as jnp
import numpy as np
from jax import lax
from jax.experimental import pallas as pl
from jax.experimental.pallas import tpu as pltpu
from jax.sharding import PartitionSpec as P

F32 = jnp.float32
BF16 = jnp.bfloat16
HIGH = lax.Precision.HIGHEST
MESH = pl.DeviceIdType.MESH
PULSES = 128
NANG = 256
BEAMS = 8
LOAD = 1e-05
DOP = 16
NX = 4
NZ = 8
RNG = NX * NZ
SIDE = 128
TR = 48
TRAIN = 1536
ROOTS = (0, 20)


def twiddles():
    angle = 2.0 * math.pi * np.arange(16) / 16
    rounded = lambda v: np.round(v, 12).astype(BF16).astype(np.float32)
    return rounded(np.cos(angle)), rounded(np.sin(angle))


def parts3(x):
    a = x.astype(BF16).astype(F32)
    r = x - a
    b = r.astype(BF16).astype(F32)
    c = (r - b).astype(BF16).astype(F32)
    return a, b, c

def left6(t):
    a, b, c = t
    return [a, a, b, a, b, c]

def right6(t):
    a, b, c = t
    return [a, b, a, c, b, a]

def neg(t):
    return tuple(-v for v in t)

def invert_block(dr, di):
    lane = lax.broadcasted_iota(jnp.int32, (8, 128), 1)
    sub = lax.broadcasted_iota(jnp.int32, (8, 128), 0)
    wide = lax.broadcasted_iota(jnp.int32, (128, 128), 1)

    def spread(v, o):
        return [jnp.broadcast_to(v[:, o+j:o+j+1], (8, 128)) for j in range(8)]

    rr, ri = dr[0:8, :], di[0:8, :]
    for p in range(16):
        o = 8 * p
        cr, ci = spread(rr, o), spread(ri, o)
        inside = (lane >= o) & (lane < o + 8)
        xr = jnp.where(inside, jnp.where(lane == o + sub, 1.0, 0.0), rr)
        xi = jnp.where(inside, 0.0, ri)
        for i in range(8):
            inv = 1.0 / cr[i][i:i+1, :]
            here = sub == i

            def step(vr, vi):
                tr = vr[i:i+1, :] * inv
                ti = vi[i:i+1, :] * inv
                nr = jnp.where(here, tr, vr - (cr[i] * tr - ci[i] * ti))
                ni = jnp.where(here, ti, vi - (cr[i] * ti + ci[i] * tr))
                return nr, ni

            for j in range(i + 1, 8):
                cr[j], ci[j] = step(cr[j], ci[j])
            xr, xi = step(xr, xi)
        if p < 15:
            br, bi = dr[o+8:o+16, :], di[o+8:o+16, :]
            er, ei = spread(br, o), spread(bi, o)
            ar, ai = [], []
            for j in range(8):
                tr, ti = xr[j:j+1, :], xi[j:j+1, :]
                ar.append(er[j] * tr - ei[j] * ti)
                ai.append(er[j] * ti + ei[j] * tr)
            while len(ar) > 1:
                ar = [a + b for a, b in zip(ar[::2], ar[1::2])]
                ai = [a + b for a, b in zip(ai[::2], ai[1::2])]
            ahead_r = jnp.where(inside, 0.0, br) - ar[0]
            ahead_i = jnp.where(inside, 0.0, bi) - ai[0]
        sign = jnp.where(lane < o, -1.0, 1.0)
        a, b = parts3(sign * rr), parts3(-sign * ri)
        left = jnp.concatenate(left6(a) + left6(b), 0).astype(BF16)
        u, v = parts3(xr), parts3(xi)
        right = jnp.concatenate([
            jnp.concatenate(right6(u) + right6(neg(v)), 0),
            jnp.concatenate(right6(v) + right6(u), 0)], 1).astype(BF16)
        upd = lax.dot_general(left, right, (((0,), (0,)), ((), ())), preferred_element_type=F32)
        hole = (wide >= o) & (wide < o + 8)
        dr[...] = jnp.where(hole, 0.0, dr[...]) - upd[:, :128]
        di[...] = jnp.where(hole, 0.0, di[...]) - upd[:, 128:]
        dr[o:o+8, :] = xr
        di[o:o+8, :] = xi
        if p < 15:
            rr, ri = ahead_r, ahead_i


def beam_kernel(cube, indices, out, got, send, even, odd, raw, spec, rows, part_d, part_r, share_d, share_r,
                sum_d, sum_r, full, steer, dr, di, row, w, x_ref, weights,
                own_sem, a_send, a_recv, b_send, b_recv, x_send, x_recv, rd_send, rd_recv, rr_send, rr_recv,
                gd_send, gd_recv, gr_send, gr_recv, w_send, w_recv):
    dop = lax.axis_index("dop")
    rng = lax.axis_index("rng")
    x, z = rng // NZ, lax.rem(rng, NZ)
    root = jnp.where(lax.rem(dop, 2) == 0, ROOTS[0], ROOTS[1])
    is_root = rng == root

    def dop_peer(step):
        return {"dop": lax.rem(dop + step, DOP)}

    def x_peer(step):
        return {"rng": lax.rem(x + step, NX) * NZ + z}

    def z_peer(step):
        return {"rng": x * NZ + lax.rem(z + step, NZ)}

    def loop(count, body, start=1):
        def one(step, carry):
            body(step)
            return carry
        lax.fori_loop(start, count, one, 0)

    def far_first(count, body):
        def one(k):
            j = count - k
            body(jnp.where(lax.rem(j, 2) == 1, (j + 1) // 2, count - j // 2))
        loop(count, one)

    def others(body):
        def one(r):
            @pl.when(r != rng)
            def _():
                body(r)
        loop(RNG, one, 0)

    barrier = pltpu.get_barrier_semaphore()

    def greet(peer):
        pl.semaphore_signal(barrier, inc=1, device_id=peer, device_id_type=MESH)

    loop(DOP, lambda step: greet(dop_peer(step)))
    aside = (root // NZ != x) & (lax.rem(root, NZ) != z)

    @pl.when(is_root)
    def _():
        loop(RNG, lambda step: greet({"rng": lax.rem(rng + step, RNG)}))

    @pl.when(jnp.logical_not(is_root))
    def _():
        loop(NX, lambda step: greet(x_peer(step)))
        loop(NZ, lambda step: greet(z_peer(step)))

    @pl.when(aside)
    def _():
        greet({"rng": root})

    near_count = DOP + NX + NZ - 3
    pl.semaphore_wait(barrier, jnp.where(is_root, DOP + RNG - 2, jnp.where(aside, near_count + 1, near_count)))

    def tile_of(index):
        return (pl.ds(pl.multiple_of(index // 4 * 16, 16), 16),
                pl.ds(pl.multiple_of(lax.rem(index, 4) * 128, 128), 128))

    def a_copy(step):
        g, c = tile_of(lax.rem(dop + step, DOP))
        return pltpu.make_async_remote_copy(
            src_ref=cube.at[:, :, g, c], dst_ref=got.at[step], send_sem=a_send.at[step],
            recv_sem=a_recv.at[step], device_id=dop_peer(step), device_id_type=MESH)

    far_first(DOP, lambda step: a_copy(step).start())
    g, c = tile_of(dop)
    own = pltpu.make_async_copy(cube.at[:, :, g, c], got.at[0], own_sem)
    own.start()

    slope = 2 * indices[1:2] + 1 - NANG
    lanes = lax.broadcasted_iota(jnp.int32, (128, 128), 1)
    for k in range(4):
        channel = lax.broadcasted_iota(jnp.int32, (128, 128), 0) + 128 * k
        turn = (channel * slope) & (2 * NANG - 1)
        phase = turn.astype(F32) * (math.pi / NANG)
        steer[0, 128*k:128*k+128, :] = jnp.where(lanes < BEAMS, jnp.cos(phase), 0.0)
        steer[1, 128*k:128*k+128, :] = jnp.where(lanes < BEAMS, jnp.sin(phase), 0.0)
    gate = lax.broadcasted_iota(jnp.int32, (64, TR), 0)
    pick = jnp.where(gate == indices[0:1, 0:TR], 1.0, 0.0).astype(BF16)

    own.wait()
    sign = jnp.where(lax.rem(dop, 2) == 0, 1.0, -1.0).astype(F32)
    first = got[0].astype(F32)
    even[...] = first
    odd[...] = sign * first

    def fold(step):
        a_copy(step).wait_recv()
        block = got[step].astype(F32)
        flip = jnp.where(lax.rem(step, 2) == 0, sign, -sign)
        even[...] += block
        odd[...] += flip * block

    loop(DOP, fold)

    cosine, sine = twiddles()
    norm = 1.0 / math.sqrt(PULSES)
    for half in range(2):
        rows8 = slice(8 * half, 8 * half + 8)
        for parity, source in enumerate((even, odd)):
            re = [source[0, q, rows8, :] for q in range(8)]
            im = [source[1, q, rows8, :] for q in range(8)]
            for b in range(parity, DOP, 2):
                up = low = None
                for q in range(8):
                    cb, sb = float(cosine[b * q % 16]), float(sine[b * q % 16])
                    for k, v in ((cb, re[q]), (sb, im[q])):
                        if k != 0.0:
                            up = k * v if up is None else up + k * v
                    for k, v in ((-sb, re[q]), (cb, im[q])):
                        if k != 0.0:
                            low = k * v if low is None else low + k * v
                raw[b, 0, rows8, :] = up * norm
                raw[b, 1, rows8, :] = low * norm
    for b in range(DOP):
        send[b] = raw[b].astype(BF16)

    def b_copy(step):
        return pltpu.make_async_remote_copy(
            src_ref=send.at[lax.rem(dop + step, DOP)], dst_ref=spec.at[:, g, c], send_sem=b_send.at[step],
            recv_sem=b_recv.at[step], device_id=dop_peer(step), device_id_type=MESH)

    far_first(DOP, lambda step: b_copy(step).start())
    spec[:, g, c] = send[dop]
    loop(DOP, lambda step: b_copy(step).wait_recv())

    for i in range(2):
        rows[0, i] = lax.dot_general(
            pick, spec[i], (((0,), (0,)), ((), ())), preferred_element_type=F32).astype(BF16)

    def x_copy(step):
        return pltpu.make_async_remote_copy(
            src_ref=rows.at[0], dst_ref=rows.at[step], send_sem=x_send.at[step],
            recv_sem=x_recv.at[step], device_id=x_peer(step), device_id_type=MESH)

    far_first(NX, lambda step: x_copy(step).start())
    loop(NX, lambda step: x_copy(step).wait_recv())

    def columns(block):
        at = pl.ds(pl.multiple_of(block * SIDE, SIDE), SIDE)
        return (rows[:, 0, :, at].reshape(NX * TR, SIDE), rows[:, 1, :, at].reshape(NX * TR, SIDE))

    def dot(a, b):
        return lax.dot_general(a, b, (((0,), (0,)), ((), ())), preferred_element_type=F32)

    def power(a, b):
        return dot(a[0], b[0]) + dot(a[1], b[1])

    def cross(a, b):
        return dot(a[0], b[1]) - dot(a[1], b[0])

    def r_copy(part, share, sends, recvs, step):
        return pltpu.make_async_remote_copy(
            src_ref=part.at[lax.rem(z + step, NZ)], dst_ref=share.at[step], send_sem=sends.at[step],
            recv_sem=recvs.at[step], device_id=z_peer(step), device_id_type=MESH)

    rd_copy = functools.partial(r_copy, part_d, share_d, rd_send, rd_recv)
    rr_copy = functools.partial(r_copy, part_r, share_r, rr_send, rr_recv)
    mine = columns(x)
    eye = lax.broadcasted_iota(jnp.int32, (SIDE, SIDE), 0) - lax.broadcasted_iota(jnp.int32, (SIDE, SIDE), 1)
    part_d[...] = jnp.where(eye >= 0, power(mine, mine), cross(mine, mine)).reshape(NZ, 16, SIDE)
    far_first(NZ, lambda step: rd_copy(step).start())
    near, far = lax.rem(x + 1, NX), lax.rem(x + 2, NX)
    low1, high1 = columns(jnp.minimum(x, near)), columns(jnp.maximum(x, near))
    low2, high2 = columns(jnp.minimum(x, far)), columns(jnp.maximum(x, far))
    part_r[:, :, 0:128] = power(low1, high1).reshape(NZ, 16, SIDE)
    part_r[:, :, 128:256] = cross(low1, high1).reshape(NZ, 16, SIDE)
    part_r[:, :, 256:384] = jnp.where(x < 2, power(low2, high2), cross(low2, high2)).reshape(NZ, 16, SIDE)
    far_first(NZ, lambda step: rr_copy(step).start())

    strip = pl.ds(pl.multiple_of(z * 16, 16), 16)

    def strip_of(r, at):
        return full.at[r // NZ, pl.ds(pl.multiple_of(lax.rem(r, NZ) * 16, 16), 16), at]

    def gd_copy(r, target):
        return pltpu.make_async_remote_copy(
            src_ref=sum_d, dst_ref=strip_of(r, slice(0, 128)), send_sem=gd_send, recv_sem=gd_recv.at[r],
            device_id={"rng": target}, device_id_type=MESH)

    def gr_copy(r, target):
        return pltpu.make_async_remote_copy(
            src_ref=sum_r, dst_ref=strip_of(r, slice(128, 512)), send_sem=gr_send, recv_sem=gr_recv.at[r],
            device_id={"rng": target}, device_id_type=MESH)

    def total(part, share, copy):
        loop(NZ, lambda step: copy(step).wait_recv())
        value = part[z]
        for step in range(1, NZ):
            value = value + share[step]
        return value * (1.0 / TRAIN)

    value_d = total(part_d, share_d, rd_copy)

    @pl.when(jnp.logical_not(is_root))
    def _():
        sum_d[...] = value_d
        gd_copy(rng, root).start()
        sum_r[...] = total(part_r, share_r, rr_copy)
        gr_copy(rng, root).start()

    def w_copy(r):
        return pltpu.make_async_remote_copy(
            src_ref=weights, dst_ref=weights, send_sem=w_send.at[r], recv_sem=w_recv,
            device_id={"rng": r}, device_id_type=MESH)

    @pl.when(is_root)
    def _():
        full[x, strip, 0:128] = value_d
        others(lambda r: gd_copy(r, root).wait_recv())
        trace = jnp.zeros((), F32)
        for i in range(4):
            trace = trace + jnp.sum(jnp.where(eye == 0, full[i, :, 0:128], 0.0))
        load = LOAD * trace / 512.0
        for i in range(4):
            t = full[i, :, 0:128]
            tt = t.T
            row[i, 0:128, 128*i:128*i+128] = jnp.where(eye > 0, t, tt) + jnp.where(eye == 0, load, 0.0)
            row[i, 128:256, 128*i:128*i+128] = jnp.where(eye > 0, tt, jnp.where(eye < 0, -t, 0.0))
            row[i, 0:128, 512:640] = steer[0, 128*i:128*i+128, :]
            row[i, 128:256, 512:640] = steer[1, 128*i:128*i+128, :]

        def rest():
            full[x, strip, 128:512] = total(part_r, share_r, rr_copy)
            others(lambda r: gr_copy(r, root).wait_recv())
            for i in range(4):
                for j in range(i + 1, 4):
                    (a, b), (e, d) = place(i, j)
                    row[i, 0:128, 128*j:128*j+128] = full[a, :, 128*b:128*b+128]
                    row[i, 128:256, 128*j:128*j+128] = -full[e, :, 128*d:128*d+128]

        solve(rest, steer, row, w, x_ref, dr, di, weights)
        others(lambda r: w_copy(r).start())

    @pl.when(jnp.logical_not(is_root))
    def _():
        w_copy(root).wait_recv()

    across = (((1,), (1,)), ((), ()))
    with_re = lax.dot_general(weights[...], spec[0], across, preferred_element_type=F32)
    with_im = lax.dot_general(weights[...], spec[1], across, preferred_element_type=F32)
    out[0] = with_re[0:8] + with_im[8:16]
    out[1] = with_re[8:16] - with_im[0:8]

    @pl.when(is_root)
    def _():
        others(lambda r: w_copy(r).wait_send())

    @pl.when(jnp.logical_not(is_root))
    def _():
        gd_copy(rng, root).wait_send()
        gr_copy(rng, root).wait_send()

    loop(DOP, lambda step: a_copy(step).wait_send())
    loop(DOP, lambda step: b_copy(step).wait_send())
    loop(NX, lambda step: x_copy(step).wait_send())
    loop(NZ, lambda step: rd_copy(step).wait_send())
    loop(NZ, lambda step: rr_copy(step).wait_send())


def place(i, j):
    if j - i == 1:
        return (i, 1), (i, 2)
    if j - i == 3:
        return (3, 1), (3, 2)
    return (i, 3), (i + 2, 3)


def solve(rest, steer, row, w, x, dr, di, weights):
    def body(k, carry):
        for kk in range(4):
            @pl.when(k == kk)
            def _():
                dr[...] = row[kk, 0:128, 128*kk:128*kk+128]
                di[...] = row[kk, 128:256, 128*kk:128*kk+128]
        invert_block(dr, di)
        for kk in range(4):
            @pl.when(k == kk)
            def _():
                if kk == 0:
                    rest()
                s = 128 * (kk + 1)
                a, b = dr[...], di[...]
                emb = jnp.concatenate([jnp.concatenate([a, -b], 1), jnp.concatenate([b, a], 1)], 0)
                w[kk, :, s:640] = jnp.dot(emb, row[kk, :, s:640], preferred_element_type=F32, precision=HIGH)
                for i in range(kk + 1, 4):
                    c = 128 * i
                    lhs = row[kk, :, c:c+128]
                    wr = w[kk, 0:128, c:640]
                    wi = w[kk, 128:256, c:640]
                    both = jnp.concatenate([jnp.concatenate([wr, wi], 1), jnp.concatenate([wi, -wr], 1)], 0)
                    n = 640 - c
                    u = lax.dot_general(lhs, both, (((0,), (0,)), ((), ())), preferred_element_type=F32, precision=HIGH)
                    row[i, 0:128, c:640] -= u[:, :n]
                    row[i, 128:256, c:640] -= u[:, n:]
        return carry

    lax.fori_loop(0, 4, body, 0)
    q = jnp.zeros((1, 128), F32)
    for k in (3, 2, 1, 0):
        y = w[k, :, 512:640]
        for j in range(k + 1, 4):
            wr = w[k, 0:128, 128*j:128*j+128]
            wi = w[k, 128:256, 128*j:128*j+128]
            emb = jnp.concatenate([jnp.concatenate([wr, -wi], 1), jnp.concatenate([wi, wr], 1)], 0)
            y = y - jnp.dot(emb, x[j], preferred_element_type=F32, precision=HIGH)
        x[k] = y
        for h in range(2):
            q = q + jnp.sum(y[128*h:128*h+128] * steer[h, 128*k:128*k+128, :], axis=0, keepdims=True)
    lanes = lax.broadcasted_iota(jnp.int32, (1, 128), 1)
    scale = lax.rsqrt(jnp.where(lanes < BEAMS, q, 1.0))
    for k in range(4):
        both = [(x[k, 128*h:128*h+128] * scale).T[0:8] for h in range(2)]
        weights[:, 128*k:128*k+128] = jnp.concatenate(both, 0).astype(BF16)


def beams(cube, indices):
    dma = pltpu.SemaphoreType.DMA
    return pl.pallas_call(
        beam_kernel,
        out_shape=jax.ShapeDtypeStruct((2, BEAMS, 64), F32),
        in_specs=[pl.BlockSpec(memory_space=pl.ANY), pl.BlockSpec(memory_space=pltpu.VMEM)],
        out_specs=pl.BlockSpec(memory_space=pltpu.VMEM),
        scratch_shapes=[
            pltpu.VMEM((DOP, 2, 8, 16, 128), BF16),
            pltpu.VMEM((DOP, 2, 16, 128), BF16),
            pltpu.VMEM((2, 8, 16, 128), F32),
            pltpu.VMEM((2, 8, 16, 128), F32),
            pltpu.VMEM((DOP, 2, 16, 128), F32),
            pltpu.VMEM((2, 64, 512), BF16),
            pltpu.VMEM((NX, 2, TR, 512), BF16),
            pltpu.VMEM((NZ, 16, 128), F32),
            pltpu.VMEM((NZ, 16, 384), F32),
            pltpu.VMEM((NZ, 16, 128), F32),
            pltpu.VMEM((NZ, 16, 384), F32),
            pltpu.VMEM((16, 128), F32),
            pltpu.VMEM((16, 384), F32),
            pltpu.VMEM((4, SIDE, 512), F32),
            pltpu.VMEM((2, 512, 128), F32),
            pltpu.VMEM((128, 128), F32),
            pltpu.VMEM((128, 128), F32),
            pltpu.VMEM((4, 256, 640), F32),
            pltpu.VMEM((4, 256, 640), F32),
            pltpu.VMEM((4, 256, 128), F32),
            pltpu.VMEM((16, 512), BF16),
            dma(()),
            dma((DOP,)), dma((DOP,)), dma((DOP,)), dma((DOP,)), dma((NX,)), dma((NX,)),
            dma((NZ,)), dma((NZ,)), dma((NZ,)), dma((NZ,)),
            dma(()), dma((RNG,)), dma(()), dma((RNG,)), dma((RNG,)), dma(()),
        ],
        compiler_params=pltpu.CompilerParams(collective_id=0, has_side_effects=True, vmem_limit_bytes=53 << 20),
        cost_estimate=pl.CostEstimate(flops=10**9, bytes_accessed=10**7, transcendentals=0),
    )(cube, indices)


def on_device(radar_cube, train_gates, look_angles):
    indices = jnp.concatenate([
        jnp.pad(train_gates, ((0, 0), (0, 128 - TR))), jnp.pad(look_angles, ((0, 0), (0, 128 - BEAMS)))], 0)
    return beams(radar_cube, indices)[:, None]


def solution(mesh):
    return jax.shard_map(
        on_device,
        mesh=mesh,
        in_specs=(P(None, "dop", "rng", None), P("dop", "rng"), P("dop", None)),
        out_specs=P(None, "dop", None, "rng"),
        check_vma=False,
    )
```

```python
import functools
import math

import jax
import jax.numpy as jnp
import numpy as np
from jax import lax
from jax.experimental import pallas as pl
from jax.experimental.pallas import tpu as pltpu
from jax.sharding import PartitionSpec as P

F32 = jnp.float32
BF16 = jnp.bfloat16
HIGH = lax.Precision.HIGHEST
MESH = pl.DeviceIdType.MESH
PULSES = 128
NANG = 256
BEAMS = 8
LOAD = 1e-05
DOP = 16
NX = 4
NZ = 8
RNG = NX * NZ
SIDE = 128
TR = 48
TRAIN = 1536
ROOTS = (0, 16)


def twiddles():
    angle = 2.0 * math.pi * np.arange(16) / 16
    rounded = lambda v: np.round(v, 12).astype(BF16).astype(np.float32)
    return rounded(np.cos(angle)), rounded(np.sin(angle))


def parts3(x):
    a = x.astype(BF16).astype(F32)
    r = x - a
    b = r.astype(BF16).astype(F32)
    c = (r - b).astype(BF16).astype(F32)
    return a, b, c

def left6(t):
    a, b, c = t
    return [a, a, b, a, b, c]

def right6(t):
    a, b, c = t
    return [a, b, a, c, b, a]

def neg(t):
    return tuple(-v for v in t)

def invert_block(dr, di):
    lane = lax.broadcasted_iota(jnp.int32, (8, 128), 1)
    sub = lax.broadcasted_iota(jnp.int32, (8, 128), 0)
    wide = lax.broadcasted_iota(jnp.int32, (128, 128), 1)

    def spread(v, o):
        return [jnp.broadcast_to(v[:, o+j:o+j+1], (8, 128)) for j in range(8)]

    rr, ri = dr[0:8, :], di[0:8, :]
    for p in range(16):
        o = 8 * p
        cr, ci = spread(rr, o), spread(ri, o)
        inside = (lane >= o) & (lane < o + 8)
        xr = jnp.where(inside, jnp.where(lane == o + sub, 1.0, 0.0), rr)
        xi = jnp.where(inside, 0.0, ri)
        for i in range(8):
            inv = 1.0 / cr[i][i:i+1, :]
            here = sub == i

            def step(vr, vi):
                tr = vr[i:i+1, :] * inv
                ti = vi[i:i+1, :] * inv
                nr = jnp.where(here, tr, vr - (cr[i] * tr - ci[i] * ti))
                ni = jnp.where(here, ti, vi - (cr[i] * ti + ci[i] * tr))
                return nr, ni

            for j in range(i + 1, 8):
                cr[j], ci[j] = step(cr[j], ci[j])
            xr, xi = step(xr, xi)
        if p < 15:
            br, bi = dr[o+8:o+16, :], di[o+8:o+16, :]
            er, ei = spread(br, o), spread(bi, o)
            ar, ai = [], []
            for j in range(8):
                tr, ti = xr[j:j+1, :], xi[j:j+1, :]
                ar.append(er[j] * tr - ei[j] * ti)
                ai.append(er[j] * ti + ei[j] * tr)
            while len(ar) > 1:
                ar = [a + b for a, b in zip(ar[::2], ar[1::2])]
                ai = [a + b for a, b in zip(ai[::2], ai[1::2])]
            ahead_r = jnp.where(inside, 0.0, br) - ar[0]
            ahead_i = jnp.where(inside, 0.0, bi) - ai[0]
        sign = jnp.where(lane < o, -1.0, 1.0)
        a, b = parts3(sign * rr), parts3(-sign * ri)
        left = jnp.concatenate(left6(a) + left6(b), 0).astype(BF16)
        u, v = parts3(xr), parts3(xi)
        right = jnp.concatenate([
            jnp.concatenate(right6(u) + right6(neg(v)), 0),
            jnp.concatenate(right6(v) + right6(u), 0)], 1).astype(BF16)
        upd = lax.dot_general(left, right, (((0,), (0,)), ((), ())), preferred_element_type=F32)
        hole = (wide >= o) & (wide < o + 8)
        dr[...] = jnp.where(hole, 0.0, dr[...]) - upd[:, :128]
        di[...] = jnp.where(hole, 0.0, di[...]) - upd[:, 128:]
        dr[o:o+8, :] = xr
        di[o:o+8, :] = xi
        if p < 15:
            rr, ri = ahead_r, ahead_i


def beam_kernel(cube, indices, out, got, send, even, odd, raw, spec, rows, part_d, part_r, share_d, share_r,
                sum_d, sum_r, full, steer, dr, di, row, w, x_ref, weights,
                own_sem, a_send, a_recv, b_send, b_recv, x_send, x_recv, rd_send, rd_recv, rr_send, rr_recv,
                gd_send, gd_recv, gr_send, gr_recv, w_send, w_recv):
    dop = lax.axis_index("dop")
    rng = lax.axis_index("rng")
    x, z = rng // NZ, lax.rem(rng, NZ)
    root = jnp.where(lax.rem(dop, 2) == 0, ROOTS[0], ROOTS[1])
    is_root = rng == root

    def dop_peer(step):
        return {"dop": lax.rem(dop + step, DOP)}

    def x_peer(step):
        return {"rng": lax.rem(x + step, NX) * NZ + z}

    def z_peer(step):
        return {"rng": x * NZ + lax.rem(z + step, NZ)}

    def loop(count, body, start=1):
        def one(step, carry):
            body(step)
            return carry
        lax.fori_loop(start, count, one, 0)

    def far_first(count, body):
        def one(k):
            j = count - k
            body(jnp.where(lax.rem(j, 2) == 1, (j + 1) // 2, count - j // 2))
        loop(count, one)

    def others(body):
        def one(i):
            r = lax.rem(i, NX) * NZ + i // NX

            @pl.when(r != rng)
            def _():
                body(r)
        loop(RNG, one, 0)

    barrier = pltpu.get_barrier_semaphore()

    def greet(peer):
        pl.semaphore_signal(barrier, inc=1, device_id=peer, device_id_type=MESH)

    loop(DOP, lambda step: greet(dop_peer(step)))
    aside = (root // NZ != x) & (lax.rem(root, NZ) != z)

    @pl.when(is_root)
    def _():
        loop(RNG, lambda step: greet({"rng": lax.rem(rng + step, RNG)}))

    @pl.when(jnp.logical_not(is_root))
    def _():
        loop(NX, lambda step: greet(x_peer(step)))
        loop(NZ, lambda step: greet(z_peer(step)))

    @pl.when(aside)
    def _():
        greet({"rng": root})

    near_count = DOP + NX + NZ - 3
    pl.semaphore_wait(barrier, jnp.where(is_root, DOP + RNG - 2, jnp.where(aside, near_count + 1, near_count)))

    def tile_of(index):
        return (pl.ds(pl.multiple_of(index // 4 * 16, 16), 16),
                pl.ds(pl.multiple_of(lax.rem(index, 4) * 128, 128), 128))

    def a_copy(step):
        g, c = tile_of(lax.rem(dop + step, DOP))
        return pltpu.make_async_remote_copy(
            src_ref=cube.at[:, :, g, c], dst_ref=got.at[step], send_sem=a_send.at[step],
            recv_sem=a_recv.at[step], device_id=dop_peer(step), device_id_type=MESH)

    far_first(DOP, lambda step: a_copy(step).start())
    g, c = tile_of(dop)
    own = pltpu.make_async_copy(cube.at[:, :, g, c], got.at[0], own_sem)
    own.start()

    slope = 2 * indices[1:2] + 1 - NANG
    lanes = lax.broadcasted_iota(jnp.int32, (128, 128), 1)
    for k in range(4):
        channel = lax.broadcasted_iota(jnp.int32, (128, 128), 0) + 128 * k
        turn = (channel * slope) & (2 * NANG - 1)
        phase = turn.astype(F32) * (math.pi / NANG)
        steer[0, 128*k:128*k+128, :] = jnp.where(lanes < BEAMS, jnp.cos(phase), 0.0)
        steer[1, 128*k:128*k+128, :] = jnp.where(lanes < BEAMS, jnp.sin(phase), 0.0)
    gate = lax.broadcasted_iota(jnp.int32, (64, TR), 0)
    pick = jnp.where(gate == indices[0:1, 0:TR], 1.0, 0.0).astype(BF16)

    own.wait()
    sign = jnp.where(lax.rem(dop, 2) == 0, 1.0, -1.0).astype(F32)
    first = got[0].astype(F32)
    even[...] = first
    odd[...] = sign * first

    def fold(step):
        a_copy(step).wait_recv()
        block = got[step].astype(F32)
        flip = jnp.where(lax.rem(step, 2) == 0, sign, -sign)
        even[...] += block
        odd[...] += flip * block

    loop(DOP, fold)

    cosine, sine = twiddles()
    norm = 1.0 / math.sqrt(PULSES)
    for half in range(2):
        rows8 = slice(8 * half, 8 * half + 8)
        for parity, source in enumerate((even, odd)):
            re = [source[0, q, rows8, :] for q in range(8)]
            im = [source[1, q, rows8, :] for q in range(8)]
            for b in range(parity, DOP, 2):
                up = low = None
                for q in range(8):
                    cb, sb = float(cosine[b * q % 16]), float(sine[b * q % 16])
                    for k, v in ((cb, re[q]), (sb, im[q])):
                        if k != 0.0:
                            up = k * v if up is None else up + k * v
                    for k, v in ((-sb, re[q]), (cb, im[q])):
                        if k != 0.0:
                            low = k * v if low is None else low + k * v
                raw[b, 0, rows8, :] = up * norm
                raw[b, 1, rows8, :] = low * norm
    for b in range(DOP):
        send[b] = raw[b].astype(BF16)

    def b_copy(step):
        return pltpu.make_async_remote_copy(
            src_ref=send.at[lax.rem(dop + step, DOP)], dst_ref=spec.at[:, g, c], send_sem=b_send.at[step],
            recv_sem=b_recv.at[step], device_id=dop_peer(step), device_id_type=MESH)

    far_first(DOP, lambda step: b_copy(step).start())
    spec[:, g, c] = send[dop]
    loop(DOP, lambda step: b_copy(step).wait_recv())

    for i in range(2):
        rows[0, i] = lax.dot_general(
            pick, spec[i], (((0,), (0,)), ((), ())), preferred_element_type=F32).astype(BF16)

    def x_copy(step):
        return pltpu.make_async_remote_copy(
            src_ref=rows.at[0], dst_ref=rows.at[step], send_sem=x_send.at[step],
            recv_sem=x_recv.at[step], device_id=x_peer(step), device_id_type=MESH)

    far_first(NX, lambda step: x_copy(step).start())
    loop(NX, lambda step: x_copy(step).wait_recv())

    def columns(block):
        at = pl.ds(pl.multiple_of(block * SIDE, SIDE), SIDE)
        return (rows[:, 0, :, at].reshape(NX * TR, SIDE), rows[:, 1, :, at].reshape(NX * TR, SIDE))

    def dot(a, b):
        return lax.dot_general(a, b, (((0,), (0,)), ((), ())), preferred_element_type=F32)

    def power(a, b):
        return dot(a[0], b[0]) + dot(a[1], b[1])

    def cross(a, b):
        return dot(a[0], b[1]) - dot(a[1], b[0])

    def r_copy(part, share, sends, recvs, step):
        return pltpu.make_async_remote_copy(
            src_ref=part.at[lax.rem(z + step, NZ)], dst_ref=share.at[step], send_sem=sends.at[step],
            recv_sem=recvs.at[step], device_id=z_peer(step), device_id_type=MESH)

    rd_copy = functools.partial(r_copy, part_d, share_d, rd_send, rd_recv)
    rr_copy = functools.partial(r_copy, part_r, share_r, rr_send, rr_recv)
    mine = columns(x)
    eye = lax.broadcasted_iota(jnp.int32, (SIDE, SIDE), 0) - lax.broadcasted_iota(jnp.int32, (SIDE, SIDE), 1)
    part_d[...] = jnp.where(eye >= 0, power(mine, mine), cross(mine, mine)).reshape(NZ, 16, SIDE)
    far_first(NZ, lambda step: rd_copy(step).start())
    near, far = lax.rem(x + 1, NX), lax.rem(x + 2, NX)
    low1, high1 = columns(jnp.minimum(x, near)), columns(jnp.maximum(x, near))
    low2, high2 = columns(jnp.minimum(x, far)), columns(jnp.maximum(x, far))
    part_r[:, :, 0:128] = power(low1, high1).reshape(NZ, 16, SIDE)
    part_r[:, :, 128:256] = cross(low1, high1).reshape(NZ, 16, SIDE)
    part_r[:, :, 256:384] = jnp.where(x < 2, power(low2, high2), cross(low2, high2)).reshape(NZ, 16, SIDE)
    far_first(NZ, lambda step: rr_copy(step).start())

    strip = pl.ds(pl.multiple_of(z * 16, 16), 16)

    def strip_of(r, at):
        return full.at[r // NZ, pl.ds(pl.multiple_of(lax.rem(r, NZ) * 16, 16), 16), at]

    def gd_copy(r, target):
        return pltpu.make_async_remote_copy(
            src_ref=sum_d, dst_ref=strip_of(r, slice(0, 128)), send_sem=gd_send, recv_sem=gd_recv.at[r],
            device_id={"rng": target}, device_id_type=MESH)

    def gr_copy(r, target):
        return pltpu.make_async_remote_copy(
            src_ref=sum_r, dst_ref=strip_of(r, slice(128, 512)), send_sem=gr_send, recv_sem=gr_recv.at[r],
            device_id={"rng": target}, device_id_type=MESH)

    def total(part, share, copy):
        loop(NZ, lambda step: copy(step).wait_recv())
        value = part[z]
        for step in range(1, NZ):
            value = value + share[step]
        return value * (1.0 / TRAIN)

    value_d = total(part_d, share_d, rd_copy)

    @pl.when(jnp.logical_not(is_root))
    def _():
        sum_d[...] = value_d
        gd_copy(rng, root).start()
        sum_r[...] = total(part_r, share_r, rr_copy)
        gr_copy(rng, root).start()

    def w_copy(r):
        return pltpu.make_async_remote_copy(
            src_ref=weights, dst_ref=weights, send_sem=w_send.at[r], recv_sem=w_recv,
            device_id={"rng": r}, device_id_type=MESH)

    @pl.when(is_root)
    def _():
        full[x, strip, 0:128] = value_d
        others(lambda r: gd_copy(r, root).wait_recv())
        trace = jnp.zeros((), F32)
        for i in range(4):
            trace = trace + jnp.sum(jnp.where(eye == 0, full[i, :, 0:128], 0.0))
        load = LOAD * trace / 512.0
        for i in range(4):
            t = full[i, :, 0:128]
            tt = t.T
            row[i, 0:128, 128*i:128*i+128] = jnp.where(eye > 0, t, tt) + jnp.where(eye == 0, load, 0.0)
            row[i, 128:256, 128*i:128*i+128] = jnp.where(eye > 0, tt, jnp.where(eye < 0, -t, 0.0))
            row[i, 0:128, 512:640] = steer[0, 128*i:128*i+128, :]
            row[i, 128:256, 512:640] = steer[1, 128*i:128*i+128, :]

        def rest():
            full[x, strip, 128:512] = total(part_r, share_r, rr_copy)
            others(lambda r: gr_copy(r, root).wait_recv())
            for i in range(4):
                for j in range(i + 1, 4):
                    (a, b), (e, d) = place(i, j)
                    row[i, 0:128, 128*j:128*j+128] = full[a, :, 128*b:128*b+128]
                    row[i, 128:256, 128*j:128*j+128] = -full[e, :, 128*d:128*d+128]

        solve(rest, steer, row, w, x_ref, dr, di, weights)
        others(lambda r: w_copy(r).start())

    @pl.when(jnp.logical_not(is_root))
    def _():
        w_copy(root).wait_recv()

    across = (((1,), (1,)), ((), ()))
    with_re = lax.dot_general(weights[...], spec[0], across, preferred_element_type=F32)
    with_im = lax.dot_general(weights[...], spec[1], across, preferred_element_type=F32)
    out[0] = with_re[0:8] + with_im[8:16]
    out[1] = with_re[8:16] - with_im[0:8]

    @pl.when(is_root)
    def _():
        others(lambda r: w_copy(r).wait_send())

    @pl.when(jnp.logical_not(is_root))
    def _():
        gd_copy(rng, root).wait_send()
        gr_copy(rng, root).wait_send()

    loop(DOP, lambda step: a_copy(step).wait_send())
    loop(DOP, lambda step: b_copy(step).wait_send())
    loop(NX, lambda step: x_copy(step).wait_send())
    loop(NZ, lambda step: rd_copy(step).wait_send())
    loop(NZ, lambda step: rr_copy(step).wait_send())


def place(i, j):
    if j - i == 1:
        return (i, 1), (i, 2)
    if j - i == 3:
        return (3, 1), (3, 2)
    return (i, 3), (i + 2, 3)


def solve(rest, steer, row, w, x, dr, di, weights):
    def body(k, carry):
        for kk in range(4):
            @pl.when(k == kk)
            def _():
                dr[...] = row[kk, 0:128, 128*kk:128*kk+128]
                di[...] = row[kk, 128:256, 128*kk:128*kk+128]
        invert_block(dr, di)
        for kk in range(4):
            @pl.when(k == kk)
            def _():
                if kk == 0:
                    rest()
                s = 128 * (kk + 1)
                a, b = dr[...], di[...]
                emb = jnp.concatenate([jnp.concatenate([a, -b], 1), jnp.concatenate([b, a], 1)], 0)
                w[kk, :, s:640] = jnp.dot(emb, row[kk, :, s:640], preferred_element_type=F32, precision=HIGH)
                for i in range(kk + 1, 4):
                    c = 128 * i
                    lhs = row[kk, :, c:c+128]
                    wr = w[kk, 0:128, c:640]
                    wi = w[kk, 128:256, c:640]
                    both = jnp.concatenate([jnp.concatenate([wr, wi], 1), jnp.concatenate([wi, -wr], 1)], 0)
                    n = 640 - c
                    u = lax.dot_general(lhs, both, (((0,), (0,)), ((), ())), preferred_element_type=F32, precision=HIGH)
                    row[i, 0:128, c:640] -= u[:, :n]
                    row[i, 128:256, c:640] -= u[:, n:]
        return carry

    lax.fori_loop(0, 4, body, 0)
    q = jnp.zeros((1, 128), F32)
    for k in (3, 2, 1, 0):
        y = w[k, :, 512:640]
        if k < 3:
            known = jnp.concatenate([
                jnp.concatenate([x[j, 0:128], x[j, 128:256]], 1) for j in range(k + 1, 4)], 0)
            u = jnp.dot(w[k, :, 128*k+128:512], known, preferred_element_type=F32, precision=HIGH)
            y = y - jnp.concatenate([
                u[0:128, 0:128] - u[128:256, 128:256], u[128:256, 0:128] + u[0:128, 128:256]], 0)
        x[k] = y
        for h in range(2):
            q = q + jnp.sum(y[128*h:128*h+128] * steer[h, 128*k:128*k+128, :], axis=0, keepdims=True)
    lanes = lax.broadcasted_iota(jnp.int32, (1, 128), 1)
    scale = lax.rsqrt(jnp.where(lanes < BEAMS, q, 1.0))
    for k in range(4):
        both = [(x[k, 128*h:128*h+128] * scale).T[0:8] for h in range(2)]
        weights[:, 128*k:128*k+128] = jnp.concatenate(both, 0).astype(BF16)


def beams(cube, indices):
    dma = pltpu.SemaphoreType.DMA
    return pl.pallas_call(
        beam_kernel,
        out_shape=jax.ShapeDtypeStruct((2, BEAMS, 64), F32),
        in_specs=[pl.BlockSpec(memory_space=pl.ANY), pl.BlockSpec(memory_space=pltpu.VMEM)],
        out_specs=pl.BlockSpec(memory_space=pltpu.VMEM),
        scratch_shapes=[
            pltpu.VMEM((DOP, 2, 8, 16, 128), BF16),
            pltpu.VMEM((DOP, 2, 16, 128), BF16),
            pltpu.VMEM((2, 8, 16, 128), F32),
            pltpu.VMEM((2, 8, 16, 128), F32),
            pltpu.VMEM((DOP, 2, 16, 128), F32),
            pltpu.VMEM((2, 64, 512), BF16),
            pltpu.VMEM((NX, 2, TR, 512), BF16),
            pltpu.VMEM((NZ, 16, 128), F32),
            pltpu.VMEM((NZ, 16, 384), F32),
            pltpu.VMEM((NZ, 16, 128), F32),
            pltpu.VMEM((NZ, 16, 384), F32),
            pltpu.VMEM((16, 128), F32),
            pltpu.VMEM((16, 384), F32),
            pltpu.VMEM((4, SIDE, 512), F32),
            pltpu.VMEM((2, 512, 128), F32),
            pltpu.VMEM((128, 128), F32),
            pltpu.VMEM((128, 128), F32),
            pltpu.VMEM((4, 256, 640), F32),
            pltpu.VMEM((4, 256, 640), F32),
            pltpu.VMEM((4, 256, 128), F32),
            pltpu.VMEM((16, 512), BF16),
            dma(()),
            dma((DOP,)), dma((DOP,)), dma((DOP,)), dma((DOP,)), dma((NX,)), dma((NX,)),
            dma((NZ,)), dma((NZ,)), dma((NZ,)), dma((NZ,)),
            dma(()), dma((RNG,)), dma(()), dma((RNG,)), dma((RNG,)), dma(()),
        ],
        compiler_params=pltpu.CompilerParams(collective_id=0, has_side_effects=True, vmem_limit_bytes=53 << 20),
        cost_estimate=pl.CostEstimate(flops=10**9, bytes_accessed=10**7, transcendentals=0),
    )(cube, indices)


def on_device(radar_cube, train_gates, look_angles):
    indices = jnp.concatenate([
        jnp.pad(train_gates, ((0, 0), (0, 128 - TR))), jnp.pad(look_angles, ((0, 0), (0, 128 - BEAMS)))], 0)
    return beams(radar_cube, indices)[:, None]


def solution(mesh):
    return jax.shard_map(
        on_device,
        mesh=mesh,
        in_specs=(P(None, "dop", "rng", None), P("dop", "rng"), P("dop", None)),
        out_specs=P(None, "dop", None, "rng"),
        check_vma=False,
    )
```

```python
import functools
import math

import jax
import jax.numpy as jnp
import numpy as np
from jax import lax
from jax.experimental import pallas as pl
from jax.experimental.pallas import tpu as pltpu
from jax.sharding import PartitionSpec as P

F32 = jnp.float32
BF16 = jnp.bfloat16
HIGH = lax.Precision.HIGHEST
MESH = pl.DeviceIdType.MESH
PULSES = 128
NANG = 256
BEAMS = 8
LOAD = 1e-05
DOP = 16
NX = 4
NZ = 8
RNG = NX * NZ
SIDE = 128
TR = 48
TRAIN = 1536
ROOTS = (0, 16)


def twiddles():
    angle = 2.0 * math.pi * np.arange(16) / 16
    rounded = lambda v: np.round(v, 12).astype(BF16).astype(np.float32)
    return rounded(np.cos(angle)), rounded(np.sin(angle))


def parts3(x):
    a = x.astype(BF16).astype(F32)
    r = x - a
    b = r.astype(BF16).astype(F32)
    c = (r - b).astype(BF16).astype(F32)
    return a, b, c

def left6(t):
    a, b, c = t
    return [a, a, b, a, b, c]

def right6(t):
    a, b, c = t
    return [a, b, a, c, b, a]

def neg(t):
    return tuple(-v for v in t)

def invert_block(dr, di):
    lane = lax.broadcasted_iota(jnp.int32, (8, 128), 1)
    sub = lax.broadcasted_iota(jnp.int32, (8, 128), 0)
    wide = lax.broadcasted_iota(jnp.int32, (128, 128), 1)

    def spread(v, o):
        return [jnp.broadcast_to(v[:, o+j:o+j+1], (8, 128)) for j in range(8)]

    rr, ri = dr[0:8, :], di[0:8, :]
    for p in range(16):
        o = 8 * p
        cr, ci = spread(rr, o), spread(ri, o)
        inside = (lane >= o) & (lane < o + 8)
        xr = jnp.where(inside, jnp.where(lane == o + sub, 1.0, 0.0), rr)
        xi = jnp.where(inside, 0.0, ri)
        for i in range(8):
            inv = 1.0 / cr[i][i:i+1, :]
            here = sub == i

            def step(vr, vi):
                tr = vr[i:i+1, :] * inv
                ti = vi[i:i+1, :] * inv
                nr = jnp.where(here, tr, vr - (cr[i] * tr - ci[i] * ti))
                ni = jnp.where(here, ti, vi - (cr[i] * ti + ci[i] * tr))
                return nr, ni

            for j in range(i + 1, 8):
                cr[j], ci[j] = step(cr[j], ci[j])
            xr, xi = step(xr, xi)
        if p < 15:
            br, bi = dr[o+8:o+16, :], di[o+8:o+16, :]
            er, ei = spread(br, o), spread(bi, o)
            ar, ai = [], []
            for j in range(8):
                tr, ti = xr[j:j+1, :], xi[j:j+1, :]
                ar.append(er[j] * tr - ei[j] * ti)
                ai.append(er[j] * ti + ei[j] * tr)
            while len(ar) > 1:
                ar = [a + b for a, b in zip(ar[::2], ar[1::2])]
                ai = [a + b for a, b in zip(ai[::2], ai[1::2])]
            ahead_r = jnp.where(inside, 0.0, br) - ar[0]
            ahead_i = jnp.where(inside, 0.0, bi) - ai[0]
        sign = jnp.where(lane < o, -1.0, 1.0)
        a, b = parts3(sign * rr), parts3(-sign * ri)
        left = jnp.concatenate(left6(a) + left6(b), 0).astype(BF16)
        u, v = parts3(xr), parts3(xi)
        right = jnp.concatenate([
            jnp.concatenate(right6(u) + right6(neg(v)), 0),
            jnp.concatenate(right6(v) + right6(u), 0)], 1).astype(BF16)
        upd = lax.dot_general(left, right, (((0,), (0,)), ((), ())), preferred_element_type=F32)
        hole = (wide >= o) & (wide < o + 8)
        dr[...] = jnp.where(hole, 0.0, dr[...]) - upd[:, :128]
        di[...] = jnp.where(hole, 0.0, di[...]) - upd[:, 128:]
        dr[o:o+8, :] = xr
        di[o:o+8, :] = xi
        if p < 15:
            rr, ri = ahead_r, ahead_i


def beam_kernel(cube, indices, out, got, send, even, odd, raw, spec, rows, part_d, part_r, share_d, share_r,
                sum_d, sum_r, full, steer, dr, di, row, w, x_ref, weights,
                own_sem, a_send, a_recv, b_send, b_recv, x_send, x_recv, rd_send, rd_recv, rr_send, rr_recv,
                gd_send, gd_recv, gr_send, gr_recv, w_send, w_recv):
    dop = lax.axis_index("dop")
    rng = lax.axis_index("rng")
    x, z = rng // NZ, lax.rem(rng, NZ)
    root = jnp.where(lax.rem(dop, 2) == 0, ROOTS[0], ROOTS[1])
    is_root = rng == root

    def dop_peer(step):
        return {"dop": lax.rem(dop + step, DOP)}

    def x_peer(step):
        return {"rng": lax.rem(x + step, NX) * NZ + z}

    def z_peer(step):
        return {"rng": x * NZ + lax.rem(z + step, NZ)}

    def loop(count, body, start=1):
        def one(step, carry):
            body(step)
            return carry
        lax.fori_loop(start, count, one, 0)

    def far_first(count, body):
        def one(k):
            j = count - k
            body(jnp.where(lax.rem(j, 2) == 1, (j + 1) // 2, count - j // 2))
        loop(count, one)

    def others(body):
        def one(i):
            r = lax.rem(i, NX) * NZ + i // NX

            @pl.when(r != rng)
            def _():
                body(r)
        loop(RNG, one, 0)

    barrier = pltpu.get_barrier_semaphore()

    def greet(peer):
        pl.semaphore_signal(barrier, inc=1, device_id=peer, device_id_type=MESH)

    loop(DOP, lambda step: greet(dop_peer(step)))
    aside = (root // NZ != x) & (lax.rem(root, NZ) != z)

    @pl.when(is_root)
    def _():
        loop(RNG, lambda step: greet({"rng": lax.rem(rng + step, RNG)}))

    @pl.when(jnp.logical_not(is_root))
    def _():
        loop(NX, lambda step: greet(x_peer(step)))
        loop(NZ, lambda step: greet(z_peer(step)))

    @pl.when(aside)
    def _():
        greet({"rng": root})

    near_count = DOP + NX + NZ - 3
    pl.semaphore_wait(barrier, jnp.where(is_root, DOP + RNG - 2, jnp.where(aside, near_count + 1, near_count)))

    def tile_of(index):
        return (pl.ds(pl.multiple_of(index // 4 * 16, 16), 16),
                pl.ds(pl.multiple_of(lax.rem(index, 4) * 128, 128), 128))

    def a_copy(step):
        g, c = tile_of(lax.rem(dop + step, DOP))
        return pltpu.make_async_remote_copy(
            src_ref=cube.at[:, :, g, c], dst_ref=got.at[step], send_sem=a_send.at[step],
            recv_sem=a_recv.at[step], device_id=dop_peer(step), device_id_type=MESH)

    far_first(DOP, lambda step: a_copy(step).start())
    g, c = tile_of(dop)
    own = pltpu.make_async_copy(cube.at[:, :, g, c], got.at[0], own_sem)
    own.start()

    slope = 2 * indices[1:2] + 1 - NANG
    lanes = lax.broadcasted_iota(jnp.int32, (128, 128), 1)
    for k in range(4):
        channel = lax.broadcasted_iota(jnp.int32, (128, 128), 0) + 128 * k
        turn = (channel * slope) & (2 * NANG - 1)
        phase = turn.astype(F32) * (math.pi / NANG)
        steer[0, 128*k:128*k+128, :] = jnp.where(lanes < BEAMS, jnp.cos(phase), 0.0)
        steer[1, 128*k:128*k+128, :] = jnp.where(lanes < BEAMS, jnp.sin(phase), 0.0)
    gate = lax.broadcasted_iota(jnp.int32, (64, TR), 0)
    pick = jnp.where(gate == indices[0:1, 0:TR], 1.0, 0.0).astype(BF16)

    own.wait()
    sign = jnp.where(lax.rem(dop, 2) == 0, 1.0, -1.0).astype(F32)
    first = got[0].astype(F32)
    even[...] = first
    odd[...] = sign * first

    def fold(step):
        a_copy(step).wait_recv()
        block = got[step].astype(F32)
        flip = jnp.where(lax.rem(step, 2) == 0, sign, -sign)
        even[...] += block
        odd[...] += flip * block

    loop(DOP, fold)

    cosine, sine = twiddles()
    norm = 1.0 / math.sqrt(PULSES)
    for half in range(2):
        rows8 = slice(8 * half, 8 * half + 8)
        for parity, source in enumerate((even, odd)):
            re = [source[0, q, rows8, :] for q in range(8)]
            im = [source[1, q, rows8, :] for q in range(8)]
            for b in range(parity, DOP, 2):
                up = low = None
                for q in range(8):
                    cb, sb = float(cosine[b * q % 16]), float(sine[b * q % 16])
                    for k, v in ((cb, re[q]), (sb, im[q])):
                        if k != 0.0:
                            up = k * v if up is None else up + k * v
                    for k, v in ((-sb, re[q]), (cb, im[q])):
                        if k != 0.0:
                            low = k * v if low is None else low + k * v
                raw[b, 0, rows8, :] = up * norm
                raw[b, 1, rows8, :] = low * norm
    for b in range(DOP):
        send[b] = raw[b].astype(BF16)

    def b_copy(step):
        return pltpu.make_async_remote_copy(
            src_ref=send.at[lax.rem(dop + step, DOP)], dst_ref=spec.at[:, g, c], send_sem=b_send.at[step],
            recv_sem=b_recv.at[step], device_id=dop_peer(step), device_id_type=MESH)

    far_first(DOP, lambda step: b_copy(step).start())
    spec[:, g, c] = send[dop]
    loop(DOP, lambda step: b_copy(step).wait_recv())

    for i in range(2):
        rows[0, i] = lax.dot_general(
            pick, spec[i], (((0,), (0,)), ((), ())), preferred_element_type=F32).astype(BF16)

    def x_copy(step):
        return pltpu.make_async_remote_copy(
            src_ref=rows.at[0], dst_ref=rows.at[step], send_sem=x_send.at[step],
            recv_sem=x_recv.at[step], device_id=x_peer(step), device_id_type=MESH)

    far_first(NX, lambda step: x_copy(step).start())
    loop(NX, lambda step: x_copy(step).wait_recv())

    def columns(block):
        at = pl.ds(pl.multiple_of(block * SIDE, SIDE), SIDE)
        return (rows[:, 0, :, at].reshape(NX * TR, SIDE), rows[:, 1, :, at].reshape(NX * TR, SIDE))

    def dot(a, b):
        return lax.dot_general(a, b, (((0,), (0,)), ((), ())), preferred_element_type=F32)

    def power(a, b):
        return dot(a[0], b[0]) + dot(a[1], b[1])

    def cross(a, b):
        return dot(a[0], b[1]) - dot(a[1], b[0])

    def r_copy(part, share, sends, recvs, step):
        return pltpu.make_async_remote_copy(
            src_ref=part.at[lax.rem(z + step, NZ)], dst_ref=share.at[step], send_sem=sends.at[step],
            recv_sem=recvs.at[step], device_id=z_peer(step), device_id_type=MESH)

    rd_copy = functools.partial(r_copy, part_d, share_d, rd_send, rd_recv)
    rr_copy = functools.partial(r_copy, part_r, share_r, rr_send, rr_recv)
    mine = columns(x)
    eye = lax.broadcasted_iota(jnp.int32, (SIDE, SIDE), 0) - lax.broadcasted_iota(jnp.int32, (SIDE, SIDE), 1)
    part_d[...] = jnp.where(eye >= 0, power(mine, mine), cross(mine, mine)).reshape(NZ, 16, SIDE)
    far_first(NZ, lambda step: rd_copy(step).start())
    near, far = lax.rem(x + 1, NX), lax.rem(x + 2, NX)
    low1, high1 = columns(jnp.minimum(x, near)), columns(jnp.maximum(x, near))
    low2, high2 = columns(jnp.minimum(x, far)), columns(jnp.maximum(x, far))
    part_r[:, :, 0:128] = power(low1, high1).reshape(NZ, 16, SIDE)
    part_r[:, :, 128:256] = cross(low1, high1).reshape(NZ, 16, SIDE)
    part_r[:, :, 256:384] = jnp.where(x < 2, power(low2, high2), cross(low2, high2)).reshape(NZ, 16, SIDE)
    far_first(NZ, lambda step: rr_copy(step).start())

    strip = pl.ds(pl.multiple_of(z * 16, 16), 16)

    def strip_of(r, at):
        return full.at[r // NZ, pl.ds(pl.multiple_of(lax.rem(r, NZ) * 16, 16), 16), at]

    def gd_copy(r, target):
        return pltpu.make_async_remote_copy(
            src_ref=sum_d, dst_ref=strip_of(r, slice(0, 128)), send_sem=gd_send, recv_sem=gd_recv.at[r],
            device_id={"rng": target}, device_id_type=MESH)

    def gr_copy(r, target):
        return pltpu.make_async_remote_copy(
            src_ref=sum_r, dst_ref=strip_of(r, slice(128, 512)), send_sem=gr_send, recv_sem=gr_recv.at[r],
            device_id={"rng": target}, device_id_type=MESH)

    def total(part, share, copy):
        loop(NZ, lambda step: copy(step).wait_recv())
        value = part[z]
        for step in range(1, NZ):
            value = value + share[step]
        return value * (1.0 / TRAIN)

    value_d = total(part_d, share_d, rd_copy)

    @pl.when(jnp.logical_not(is_root))
    def _():
        sum_d[...] = value_d
        gd_copy(rng, root).start()
        sum_r[...] = total(part_r, share_r, rr_copy)
        gr_copy(rng, root).start()

    before = lax.rem(root + NZ - 1, NZ)
    relays = z == before

    def along_x(step):
        return lax.rem(x + step, NX) * NZ + z

    def along_z(step):
        return x * NZ + lax.rem(z + step, NZ)

    def w_copy(r):
        return pltpu.make_async_remote_copy(
            src_ref=weights, dst_ref=weights, send_sem=w_send.at[r], recv_sem=w_recv,
            device_id={"rng": r}, device_id_type=MESH)

    @pl.when(is_root)
    def _():
        full[x, strip, 0:128] = value_d
        others(lambda r: gd_copy(r, root).wait_recv())
        trace = jnp.zeros((), F32)
        for i in range(4):
            trace = trace + jnp.sum(jnp.where(eye == 0, full[i, :, 0:128], 0.0))
        load = LOAD * trace / 512.0
        for i in range(4):
            t = full[i, :, 0:128]
            tt = t.T
            row[i, 0:128, 128*i:128*i+128] = jnp.where(eye > 0, t, tt) + jnp.where(eye == 0, load, 0.0)
            row[i, 128:256, 128*i:128*i+128] = jnp.where(eye > 0, tt, jnp.where(eye < 0, -t, 0.0))
            row[i, 0:128, 512:640] = steer[0, 128*i:128*i+128, :]
            row[i, 128:256, 512:640] = steer[1, 128*i:128*i+128, :]

        def rest():
            full[x, strip, 128:512] = total(part_r, share_r, rr_copy)
            others(lambda r: gr_copy(r, root).wait_recv())
            for i in range(4):
                for j in range(i + 1, 4):
                    (a, b), (e, d) = place(i, j)
                    row[i, 0:128, 128*j:128*j+128] = full[a, :, 128*b:128*b+128]
                    row[i, 128:256, 128*j:128*j+128] = -full[e, :, 128*d:128*d+128]

        solve(rest, steer, row, w, x_ref, dr, di, weights)
        loop(NX, lambda step: w_copy(along_x(step)).start())
        for ahead in (1, NZ - 1, 2):
            loop(NX, lambda column: w_copy(column * NZ + lax.rem(root + ahead, NZ)).start(), 0)

    @pl.when(jnp.logical_not(is_root))
    def _():
        w_copy(root).wait_recv()

    @pl.when(relays)
    def _():
        loop(NZ, lambda step: w_copy(along_z(step)).start(), 4)

    across = (((1,), (1,)), ((), ()))
    with_re = lax.dot_general(weights[...], spec[0], across, preferred_element_type=F32)
    with_im = lax.dot_general(weights[...], spec[1], across, preferred_element_type=F32)
    out[0] = with_re[0:8] + with_im[8:16]
    out[1] = with_re[8:16] - with_im[0:8]

    @pl.when(is_root)
    def _():
        loop(NX, lambda step: w_copy(along_x(step)).wait_send())
        for ahead in (1, NZ - 1, 2):
            loop(NX, lambda column: w_copy(column * NZ + lax.rem(root + ahead, NZ)).wait_send(), 0)

    @pl.when(relays)
    def _():
        loop(NZ, lambda step: w_copy(along_z(step)).wait_send(), 4)

    @pl.when(jnp.logical_not(is_root))
    def _():
        gd_copy(rng, root).wait_send()
        gr_copy(rng, root).wait_send()

    loop(DOP, lambda step: a_copy(step).wait_send())
    loop(DOP, lambda step: b_copy(step).wait_send())
    loop(NX, lambda step: x_copy(step).wait_send())
    loop(NZ, lambda step: rd_copy(step).wait_send())
    loop(NZ, lambda step: rr_copy(step).wait_send())


def place(i, j):
    if j - i == 1:
        return (i, 1), (i, 2)
    if j - i == 3:
        return (3, 1), (3, 2)
    return (i, 3), (i + 2, 3)


def solve(rest, steer, row, w, x, dr, di, weights):
    def body(k, carry):
        for kk in range(4):
            @pl.when(k == kk)
            def _():
                dr[...] = row[kk, 0:128, 128*kk:128*kk+128]
                di[...] = row[kk, 128:256, 128*kk:128*kk+128]
        invert_block(dr, di)
        for kk in range(4):
            @pl.when(k == kk)
            def _():
                if kk == 0:
                    rest()
                s = 128 * (kk + 1)
                a, b = dr[...], di[...]
                emb = jnp.concatenate([jnp.concatenate([a, -b], 1), jnp.concatenate([b, a], 1)], 0)
                w[kk, :, s:640] = jnp.dot(emb, row[kk, :, s:640], preferred_element_type=F32, precision=HIGH)
                for i in range(kk + 1, 4):
                    c = 128 * i
                    lhs = row[kk, :, c:c+128]
                    wr = w[kk, 0:128, c:640]
                    wi = w[kk, 128:256, c:640]
                    both = jnp.concatenate([jnp.concatenate([wr, wi], 1), jnp.concatenate([wi, -wr], 1)], 0)
                    n = 640 - c
                    u = lax.dot_general(lhs, both, (((0,), (0,)), ((), ())), preferred_element_type=F32, precision=HIGH)
                    row[i, 0:128, c:640] -= u[:, :n]
                    row[i, 128:256, c:640] -= u[:, n:]
        return carry

    lax.fori_loop(0, 4, body, 0)
    q = jnp.zeros((1, 128), F32)
    for k in (3, 2, 1, 0):
        y = w[k, :, 512:640]
        if k < 3:
            known = jnp.concatenate([
                jnp.concatenate([x[j, 0:128], x[j, 128:256]], 1) for j in range(k + 1, 4)], 0)
            u = jnp.dot(w[k, :, 128*k+128:512], known, preferred_element_type=F32, precision=HIGH)
            y = y - jnp.concatenate([
                u[0:128, 0:128] - u[128:256, 128:256], u[128:256, 0:128] + u[0:128, 128:256]], 0)
        x[k] = y
        for h in range(2):
            q = q + jnp.sum(y[128*h:128*h+128] * steer[h, 128*k:128*k+128, :], axis=0, keepdims=True)
    lanes = lax.broadcasted_iota(jnp.int32, (1, 128), 1)
    scale = lax.rsqrt(jnp.where(lanes < BEAMS, q, 1.0))
    for k in range(4):
        both = [(x[k, 128*h:128*h+128] * scale).T[0:8] for h in range(2)]
        weights[:, 128*k:128*k+128] = jnp.concatenate(both, 0).astype(BF16)


def beams(cube, indices):
    dma = pltpu.SemaphoreType.DMA
    return pl.pallas_call(
        beam_kernel,
        out_shape=jax.ShapeDtypeStruct((2, BEAMS, 64), F32),
        in_specs=[pl.BlockSpec(memory_space=pl.ANY), pl.BlockSpec(memory_space=pltpu.VMEM)],
        out_specs=pl.BlockSpec(memory_space=pltpu.VMEM),
        scratch_shapes=[
            pltpu.VMEM((DOP, 2, 8, 16, 128), BF16),
            pltpu.VMEM((DOP, 2, 16, 128), BF16),
            pltpu.VMEM((2, 8, 16, 128), F32),
            pltpu.VMEM((2, 8, 16, 128), F32),
            pltpu.VMEM((DOP, 2, 16, 128), F32),
            pltpu.VMEM((2, 64, 512), BF16),
            pltpu.VMEM((NX, 2, TR, 512), BF16),
            pltpu.VMEM((NZ, 16, 128), F32),
            pltpu.VMEM((NZ, 16, 384), F32),
            pltpu.VMEM((NZ, 16, 128), F32),
            pltpu.VMEM((NZ, 16, 384), F32),
            pltpu.VMEM((16, 128), F32),
            pltpu.VMEM((16, 384), F32),
            pltpu.VMEM((4, SIDE, 512), F32),
            pltpu.VMEM((2, 512, 128), F32),
            pltpu.VMEM((128, 128), F32),
            pltpu.VMEM((128, 128), F32),
            pltpu.VMEM((4, 256, 640), F32),
            pltpu.VMEM((4, 256, 640), F32),
            pltpu.VMEM((4, 256, 128), F32),
            pltpu.VMEM((16, 512), BF16),
            dma(()),
            dma((DOP,)), dma((DOP,)), dma((DOP,)), dma((DOP,)), dma((NX,)), dma((NX,)),
            dma((NZ,)), dma((NZ,)), dma((NZ,)), dma((NZ,)),
            dma(()), dma((RNG,)), dma(()), dma((RNG,)), dma((RNG,)), dma(()),
        ],
        compiler_params=pltpu.CompilerParams(collective_id=0, has_side_effects=True, vmem_limit_bytes=53 << 20),
        cost_estimate=pl.CostEstimate(flops=10**9, bytes_accessed=10**7, transcendentals=0),
    )(cube, indices)


def on_device(radar_cube, train_gates, look_angles):
    indices = jnp.concatenate([
        jnp.pad(train_gates, ((0, 0), (0, 128 - TR))), jnp.pad(look_angles, ((0, 0), (0, 128 - BEAMS)))], 0)
    return beams(radar_cube, indices)[:, None]


def solution(mesh):
    return jax.shard_map(
        on_device,
        mesh=mesh,
        in_specs=(P(None, "dop", "rng", None), P("dop", "rng"), P("dop", None)),
        out_specs=P(None, "dop", None, "rng"),
        check_vma=False,
    )
```

```python
import functools
import math

import jax
import jax.numpy as jnp
import numpy as np
from jax import lax
from jax.experimental import pallas as pl
from jax.experimental.pallas import tpu as pltpu
from jax.sharding import PartitionSpec as P

F32 = jnp.float32
BF16 = jnp.bfloat16
HIGH = lax.Precision.HIGHEST
MESH = pl.DeviceIdType.MESH
PULSES = 128
NANG = 256
BEAMS = 8
LOAD = 1e-05
DOP = 16
NX = 4
NZ = 8
RNG = NX * NZ
SIDE = 128
TR = 48
TRAIN = 1536
ROOTS = (0, 16)


def twiddles():
    angle = 2.0 * math.pi * np.arange(16) / 16
    rounded = lambda v: np.round(v, 12).astype(BF16).astype(np.float32)
    return rounded(np.cos(angle)), rounded(np.sin(angle))


def parts3(x):
    a = x.astype(BF16).astype(F32)
    r = x - a
    b = r.astype(BF16).astype(F32)
    c = (r - b).astype(BF16).astype(F32)
    return a, b, c

def left6(t):
    a, b, c = t
    return [a, a, b, a, b, c]

def right6(t):
    a, b, c = t
    return [a, b, a, c, b, a]

def neg(t):
    return tuple(-v for v in t)

def invert_block(dr, di):
    lane = lax.broadcasted_iota(jnp.int32, (8, 128), 1)
    sub = lax.broadcasted_iota(jnp.int32, (8, 128), 0)
    wide = lax.broadcasted_iota(jnp.int32, (128, 128), 1)

    def spread(v, o):
        return [jnp.broadcast_to(v[:, o+j:o+j+1], (8, 128)) for j in range(8)]

    rr, ri = dr[0:8, :], di[0:8, :]
    for p in range(16):
        o = 8 * p
        cr, ci = spread(rr, o), spread(ri, o)
        inside = (lane >= o) & (lane < o + 8)
        xr = jnp.where(inside, jnp.where(lane == o + sub, 1.0, 0.0), rr)
        xi = jnp.where(inside, 0.0, ri)
        for i in range(8):
            inv = 1.0 / cr[i][i:i+1, :]
            here = sub == i

            def step(vr, vi):
                tr = vr[i:i+1, :] * inv
                ti = vi[i:i+1, :] * inv
                nr = jnp.where(here, tr, vr - (cr[i] * tr - ci[i] * ti))
                ni = jnp.where(here, ti, vi - (cr[i] * ti + ci[i] * tr))
                return nr, ni

            for j in range(i + 1, 8):
                cr[j], ci[j] = step(cr[j], ci[j])
            xr, xi = step(xr, xi)
        if p < 15:
            br, bi = dr[o+8:o+16, :], di[o+8:o+16, :]
            er, ei = spread(br, o), spread(bi, o)
            ar, ai = [], []
            for j in range(8):
                tr, ti = xr[j:j+1, :], xi[j:j+1, :]
                ar.append(er[j] * tr - ei[j] * ti)
                ai.append(er[j] * ti + ei[j] * tr)
            while len(ar) > 1:
                ar = [a + b for a, b in zip(ar[::2], ar[1::2])]
                ai = [a + b for a, b in zip(ai[::2], ai[1::2])]
            ahead_r = jnp.where(inside, 0.0, br) - ar[0]
            ahead_i = jnp.where(inside, 0.0, bi) - ai[0]
        sign = jnp.where(lane < o, -1.0, 1.0)
        a, b = parts3(sign * rr), parts3(-sign * ri)
        left = jnp.concatenate(left6(a) + left6(b), 0).astype(BF16)
        u, v = parts3(xr), parts3(xi)
        right = jnp.concatenate([
            jnp.concatenate(right6(u) + right6(neg(v)), 0),
            jnp.concatenate(right6(v) + right6(u), 0)], 1).astype(BF16)
        upd = lax.dot_general(left, right, (((0,), (0,)), ((), ())), preferred_element_type=F32)
        hole = (wide >= o) & (wide < o + 8)
        dr[...] = jnp.where(hole, 0.0, dr[...]) - upd[:, :128]
        di[...] = jnp.where(hole, 0.0, di[...]) - upd[:, 128:]
        dr[o:o+8, :] = xr
        di[o:o+8, :] = xi
        if p < 15:
            rr, ri = ahead_r, ahead_i


def beam_kernel(cube, indices, out, got, send, even, odd, raw, spec, rows, part_d, part_r, share_d, share_r,
                sum_d, sum_r, full, steer, dr, di, row, w, x_ref, weights,
                own_sem, a_send, a_recv, b_send, b_recv, x_send, x_recv, rd_send, rd_recv, rr_send, rr_recv,
                gd_send, gd_recv, gr_send, gr_recv, w_send, w_recv):
    dop = lax.axis_index("dop")
    rng = lax.axis_index("rng")
    x, z = rng // NZ, lax.rem(rng, NZ)
    root = jnp.where(lax.rem(dop, 2) == 0, ROOTS[0], ROOTS[1])
    is_root = rng == root

    def dop_peer(step):
        return {"dop": lax.rem(dop + step, DOP)}

    def x_peer(step):
        return {"rng": lax.rem(x + step, NX) * NZ + z}

    def z_peer(step):
        return {"rng": x * NZ + lax.rem(z + step, NZ)}

    def loop(count, body, start=1):
        def one(step, carry):
            body(step)
            return carry
        lax.fori_loop(start, count, one, 0)

    def far_first(count, body):
        def one(k):
            j = count - k
            body(jnp.where(lax.rem(j, 2) == 1, (j + 1) // 2, count - j // 2))
        loop(count, one)

    def others(body):
        def one(i):
            r = lax.rem(i, NX) * NZ + i // NX

            @pl.when(r != rng)
            def _():
                body(r)
        loop(RNG, one, 0)

    barrier = pltpu.get_barrier_semaphore()

    def greet(peer):
        pl.semaphore_signal(barrier, inc=1, device_id=peer, device_id_type=MESH)

    loop(DOP, lambda step: greet(dop_peer(step)))
    aside = (root // NZ != x) & (lax.rem(root, NZ) != z)

    @pl.when(is_root)
    def _():
        loop(RNG, lambda step: greet({"rng": lax.rem(rng + step, RNG)}))

    @pl.when(jnp.logical_not(is_root))
    def _():
        loop(NX, lambda step: greet(x_peer(step)))
        loop(NZ, lambda step: greet(z_peer(step)))

    @pl.when(aside)
    def _():
        greet({"rng": root})

    near_count = DOP + NX + NZ - 3
    pl.semaphore_wait(barrier, jnp.where(is_root, DOP + RNG - 2, jnp.where(aside, near_count + 1, near_count)))

    def tile_of(index):
        return (pl.ds(pl.multiple_of(index // 4 * 16, 16), 16),
                pl.ds(pl.multiple_of(lax.rem(index, 4) * 128, 128), 128))

    def a_copy(step):
        g, c = tile_of(lax.rem(dop + step, DOP))
        return pltpu.make_async_remote_copy(
            src_ref=cube.at[:, :, g, c], dst_ref=got.at[step], send_sem=a_send.at[step],
            recv_sem=a_recv.at[step], device_id=dop_peer(step), device_id_type=MESH)

    far_first(DOP, lambda step: a_copy(step).start())
    g, c = tile_of(dop)
    own = pltpu.make_async_copy(cube.at[:, :, g, c], got.at[0], own_sem)
    own.start()

    slope = 2 * indices[1:2] + 1 - NANG
    lanes = lax.broadcasted_iota(jnp.int32, (128, 128), 1)
    for k in range(4):
        channel = lax.broadcasted_iota(jnp.int32, (128, 128), 0) + 128 * k
        turn = (channel * slope) & (2 * NANG - 1)
        phase = turn.astype(F32) * (math.pi / NANG)
        steer[0, 128*k:128*k+128, :] = jnp.where(lanes < BEAMS, jnp.cos(phase), 0.0)
        steer[1, 128*k:128*k+128, :] = jnp.where(lanes < BEAMS, jnp.sin(phase), 0.0)
        row[k, 0:128, 512:640] = steer[0, 128*k:128*k+128, :]
        row[k, 128:256, 512:640] = steer[1, 128*k:128*k+128, :]
    gate = lax.broadcasted_iota(jnp.int32, (64, TR), 0)
    pick = jnp.where(gate == indices[0:1, 0:TR], 1.0, 0.0).astype(BF16)

    own.wait()
    sign = jnp.where(lax.rem(dop, 2) == 0, 1.0, -1.0).astype(F32)
    first = got[0].astype(F32)
    even[...] = first
    odd[...] = sign * first

    def fold(step):
        a_copy(step).wait_recv()
        block = got[step].astype(F32)
        flip = jnp.where(lax.rem(step, 2) == 0, sign, -sign)
        even[...] += block
        odd[...] += flip * block

    loop(DOP, fold)

    cosine, sine = twiddles()
    norm = 1.0 / math.sqrt(PULSES)
    for half in range(2):
        rows8 = slice(8 * half, 8 * half + 8)
        for parity, source in enumerate((even, odd)):
            re = [source[0, q, rows8, :] for q in range(8)]
            im = [source[1, q, rows8, :] for q in range(8)]
            for b in range(parity, DOP, 2):
                up = low = None
                for q in range(8):
                    cb, sb = float(cosine[b * q % 16]), float(sine[b * q % 16])
                    for k, v in ((cb, re[q]), (sb, im[q])):
                        if k != 0.0:
                            up = k * v if up is None else up + k * v
                    for k, v in ((-sb, re[q]), (cb, im[q])):
                        if k != 0.0:
                            low = k * v if low is None else low + k * v
                raw[b, 0, rows8, :] = up * norm
                raw[b, 1, rows8, :] = low * norm
    for b in range(DOP):
        send[b] = raw[b].astype(BF16)

    def b_copy(step):
        return pltpu.make_async_remote_copy(
            src_ref=send.at[lax.rem(dop + step, DOP)], dst_ref=spec.at[:, g, c], send_sem=b_send.at[step],
            recv_sem=b_recv.at[step], device_id=dop_peer(step), device_id_type=MESH)

    far_first(DOP, lambda step: b_copy(step).start())
    spec[:, g, c] = send[dop]
    loop(DOP, lambda step: b_copy(step).wait_recv())

    for i in range(2):
        rows[0, i] = lax.dot_general(
            pick, spec[i], (((0,), (0,)), ((), ())), preferred_element_type=F32).astype(BF16)

    def x_copy(step):
        return pltpu.make_async_remote_copy(
            src_ref=rows.at[0], dst_ref=rows.at[step], send_sem=x_send.at[step],
            recv_sem=x_recv.at[step], device_id=x_peer(step), device_id_type=MESH)

    far_first(NX, lambda step: x_copy(step).start())
    loop(NX, lambda step: x_copy(step).wait_recv())

    def columns(block):
        at = pl.ds(pl.multiple_of(block * SIDE, SIDE), SIDE)
        return (rows[:, 0, :, at].reshape(NX * TR, SIDE), rows[:, 1, :, at].reshape(NX * TR, SIDE))

    def dot(a, b):
        return lax.dot_general(a, b, (((0,), (0,)), ((), ())), preferred_element_type=F32)

    def power(a, b):
        return dot(a[0], b[0]) + dot(a[1], b[1])

    def cross(a, b):
        return dot(a[0], b[1]) - dot(a[1], b[0])

    def r_copy(part, share, sends, recvs, step):
        return pltpu.make_async_remote_copy(
            src_ref=part.at[lax.rem(z + step, NZ)], dst_ref=share.at[step], send_sem=sends.at[step],
            recv_sem=recvs.at[step], device_id=z_peer(step), device_id_type=MESH)

    rd_copy = functools.partial(r_copy, part_d, share_d, rd_send, rd_recv)
    rr_copy = functools.partial(r_copy, part_r, share_r, rr_send, rr_recv)
    mine = columns(x)
    eye = lax.broadcasted_iota(jnp.int32, (SIDE, SIDE), 0) - lax.broadcasted_iota(jnp.int32, (SIDE, SIDE), 1)
    part_d[...] = jnp.where(eye >= 0, power(mine, mine), cross(mine, mine)).reshape(NZ, 16, SIDE)
    far_first(NZ, lambda step: rd_copy(step).start())
    near, far = lax.rem(x + 1, NX), lax.rem(x + 2, NX)
    low1, high1 = columns(jnp.minimum(x, near)), columns(jnp.maximum(x, near))
    low2, high2 = columns(jnp.minimum(x, far)), columns(jnp.maximum(x, far))
    part_r[:, :, 0:128] = power(low1, high1).reshape(NZ, 16, SIDE)
    part_r[:, :, 128:256] = cross(low1, high1).reshape(NZ, 16, SIDE)
    part_r[:, :, 256:384] = jnp.where(x < 2, power(low2, high2), cross(low2, high2)).reshape(NZ, 16, SIDE)
    far_first(NZ, lambda step: rr_copy(step).start())

    strip = pl.ds(pl.multiple_of(z * 16, 16), 16)

    def strip_of(r, at):
        return full.at[r // NZ, pl.ds(pl.multiple_of(lax.rem(r, NZ) * 16, 16), 16), at]

    def gd_copy(r, target):
        return pltpu.make_async_remote_copy(
            src_ref=sum_d, dst_ref=strip_of(r, slice(0, 128)), send_sem=gd_send, recv_sem=gd_recv.at[r],
            device_id={"rng": target}, device_id_type=MESH)

    def gr_copy(r, target):
        return pltpu.make_async_remote_copy(
            src_ref=sum_r, dst_ref=strip_of(r, slice(128, 512)), send_sem=gr_send, recv_sem=gr_recv.at[r],
            device_id={"rng": target}, device_id_type=MESH)

    def total(part, share, copy):
        loop(NZ, lambda step: copy(step).wait_recv())
        value = part[z]
        for step in range(1, NZ):
            value = value + share[step]
        return value * (1.0 / TRAIN)

    value_d = total(part_d, share_d, rd_copy)

    @pl.when(jnp.logical_not(is_root))
    def _():
        sum_d[...] = value_d
        gd_copy(rng, root).start()
        sum_r[...] = total(part_r, share_r, rr_copy)
        gr_copy(rng, root).start()

    def w_copy(r):
        return pltpu.make_async_remote_copy(
            src_ref=weights, dst_ref=weights, send_sem=w_send.at[r], recv_sem=w_recv,
            device_id={"rng": r}, device_id_type=MESH)

    @pl.when(is_root)
    def _():
        full[x, strip, 0:128] = value_d
        others(lambda r: gd_copy(r, root).wait_recv())
        trace = jnp.zeros((), F32)
        for i in range(4):
            trace = trace + jnp.sum(jnp.where(eye == 0, full[i, :, 0:128], 0.0))
        load = LOAD * trace / 512.0
        for i in range(4):
            t = full[i, :, 0:128]
            tt = t.T
            row[i, 0:128, 128*i:128*i+128] = jnp.where(eye > 0, t, tt) + jnp.where(eye == 0, load, 0.0)
            row[i, 128:256, 128*i:128*i+128] = jnp.where(eye > 0, tt, jnp.where(eye < 0, -t, 0.0))

        def rest():
            full[x, strip, 128:512] = total(part_r, share_r, rr_copy)
            others(lambda r: gr_copy(r, root).wait_recv())
            for i in range(4):
                for j in range(i + 1, 4):
                    (a, b), (e, d) = place(i, j)
                    row[i, 0:128, 128*j:128*j+128] = full[a, :, 128*b:128*b+128]
                    row[i, 128:256, 128*j:128*j+128] = -full[e, :, 128*d:128*d+128]

        solve(rest, steer, row, w, x_ref, dr, di, weights)
        others(lambda r: w_copy(r).start())

    @pl.when(jnp.logical_not(is_root))
    def _():
        w_copy(root).wait_recv()

    across = (((1,), (1,)), ((), ()))
    with_re = lax.dot_general(weights[...], spec[0], across, preferred_element_type=F32)
    with_im = lax.dot_general(weights[...], spec[1], across, preferred_element_type=F32)
    out[0] = with_re[0:8] + with_im[8:16]
    out[1] = with_re[8:16] - with_im[0:8]

    @pl.when(is_root)
    def _():
        others(lambda r: w_copy(r).wait_send())

    @pl.when(jnp.logical_not(is_root))
    def _():
        gd_copy(rng, root).wait_send()
        gr_copy(rng, root).wait_send()

    loop(DOP, lambda step: a_copy(step).wait_send())
    loop(DOP, lambda step: b_copy(step).wait_send())
    loop(NX, lambda step: x_copy(step).wait_send())
    loop(NZ, lambda step: rd_copy(step).wait_send())
    loop(NZ, lambda step: rr_copy(step).wait_send())


def place(i, j):
    if j - i == 1:
        return (i, 1), (i, 2)
    if j - i == 3:
        return (3, 1), (3, 2)
    return (i, 3), (i + 2, 3)


def solve(rest, steer, row, w, x, dr, di, weights):
    def body(k, carry):
        for kk in range(4):
            @pl.when(k == kk)
            def _():
                dr[...] = row[kk, 0:128, 128*kk:128*kk+128]
                di[...] = row[kk, 128:256, 128*kk:128*kk+128]
        invert_block(dr, di)
        for kk in range(4):
            @pl.when(k == kk)
            def _():
                if kk == 0:
                    rest()
                s = 128 * (kk + 1)
                a, b = dr[...], di[...]
                emb = jnp.concatenate([jnp.concatenate([a, -b], 1), jnp.concatenate([b, a], 1)], 0)
                w[kk, :, s:640] = jnp.dot(emb, row[kk, :, s:640], preferred_element_type=F32, precision=HIGH)
                for i in range(kk + 1, 4):
                    c = 128 * i
                    lhs = row[kk, :, c:c+128]
                    wr = w[kk, 0:128, c:640]
                    wi = w[kk, 128:256, c:640]
                    both = jnp.concatenate([jnp.concatenate([wr, wi], 1), jnp.concatenate([wi, -wr], 1)], 0)
                    n = 640 - c
                    u = lax.dot_general(lhs, both, (((0,), (0,)), ((), ())), preferred_element_type=F32, precision=HIGH)
                    row[i, 0:128, c:640] -= u[:, :n]
                    row[i, 128:256, c:640] -= u[:, n:]
        return carry

    lax.fori_loop(0, 4, body, 0)
    q = jnp.zeros((1, 128), F32)
    for k in (3, 2, 1, 0):
        y = w[k, :, 512:640]
        if k < 3:
            known = jnp.concatenate([
                jnp.concatenate([x[j, 0:128], x[j, 128:256]], 1) for j in range(k + 1, 4)], 0)
            u = jnp.dot(w[k, :, 128*k+128:512], known, preferred_element_type=F32, precision=HIGH)
            y = y - jnp.concatenate([
                u[0:128, 0:128] - u[128:256, 128:256], u[128:256, 0:128] + u[0:128, 128:256]], 0)
        x[k] = y
        for h in range(2):
            q = q + jnp.sum(y[128*h:128*h+128] * steer[h, 128*k:128*k+128, :], axis=0, keepdims=True)
    lanes = lax.broadcasted_iota(jnp.int32, (1, 128), 1)
    scale = lax.rsqrt(jnp.where(lanes < BEAMS, q, 1.0))
    for k in range(4):
        both = [(x[k, 128*h:128*h+128] * scale).T[0:8] for h in range(2)]
        weights[:, 128*k:128*k+128] = jnp.concatenate(both, 0).astype(BF16)


def beams(cube, indices):
    dma = pltpu.SemaphoreType.DMA
    return pl.pallas_call(
        beam_kernel,
        out_shape=jax.ShapeDtypeStruct((2, BEAMS, 64), F32),
        in_specs=[pl.BlockSpec(memory_space=pl.ANY), pl.BlockSpec(memory_space=pltpu.VMEM)],
        out_specs=pl.BlockSpec(memory_space=pltpu.VMEM),
        scratch_shapes=[
            pltpu.VMEM((DOP, 2, 8, 16, 128), BF16),
            pltpu.VMEM((DOP, 2, 16, 128), BF16),
            pltpu.VMEM((2, 8, 16, 128), F32),
            pltpu.VMEM((2, 8, 16, 128), F32),
            pltpu.VMEM((DOP, 2, 16, 128), F32),
            pltpu.VMEM((2, 64, 512), BF16),
            pltpu.VMEM((NX, 2, TR, 512), BF16),
            pltpu.VMEM((NZ, 16, 128), F32),
            pltpu.VMEM((NZ, 16, 384), F32),
            pltpu.VMEM((NZ, 16, 128), F32),
            pltpu.VMEM((NZ, 16, 384), F32),
            pltpu.VMEM((16, 128), F32),
            pltpu.VMEM((16, 384), F32),
            pltpu.VMEM((4, SIDE, 512), F32),
            pltpu.VMEM((2, 512, 128), F32),
            pltpu.VMEM((128, 128), F32),
            pltpu.VMEM((128, 128), F32),
            pltpu.VMEM((4, 256, 640), F32),
            pltpu.VMEM((4, 256, 640), F32),
            pltpu.VMEM((4, 256, 128), F32),
            pltpu.VMEM((16, 512), BF16),
            dma(()),
            dma((DOP,)), dma((DOP,)), dma((DOP,)), dma((DOP,)), dma((NX,)), dma((NX,)),
            dma((NZ,)), dma((NZ,)), dma((NZ,)), dma((NZ,)),
            dma(()), dma((RNG,)), dma(()), dma((RNG,)), dma((RNG,)), dma(()),
        ],
        compiler_params=pltpu.CompilerParams(collective_id=0, has_side_effects=True, vmem_limit_bytes=53 << 20),
        cost_estimate=pl.CostEstimate(flops=10**9, bytes_accessed=10**7, transcendentals=0),
    )(cube, indices)


def on_device(radar_cube, train_gates, look_angles):
    indices = jnp.concatenate([
        jnp.pad(train_gates, ((0, 0), (0, 128 - TR))), jnp.pad(look_angles, ((0, 0), (0, 128 - BEAMS)))], 0)
    return beams(radar_cube, indices)[:, None]


def solution(mesh):
    return jax.shard_map(
        on_device,
        mesh=mesh,
        in_specs=(P(None, "dop", "rng", None), P("dop", "rng"), P("dop", None)),
        out_specs=P(None, "dop", None, "rng"),
        check_vma=False,
    )
```
